512 devices in a mesh: pipe: 8 (over z), expert: 64 (over x, y, core).
Axes of the slice: x: 4, y: 8, z: 8, core: 2. Of those that a mesh axis runs over, the one named last changes fastest.
Arguments:
- state_down: bfloat16 [8, 1024, 3584], P('pipe', 'expert'), may hold values from -6 to 6
- state_up: bfloat16 [8, 1024, 3584], P('pipe', 'expert'), may hold values from -6 to 6
- routes: int32 [1, 8, 2, 1024, 2], P(None, 'pipe', None, 'expert'), may hold values from 0 to 7, all different within a row; in each aligned block of 16 rows (0 to 15, 16 to 31, ..., all dimensions but the last counted through in order) at most 8 rows name the same one
- gains: float32 [8, 2, 3584], P('pipe'), may hold values from 0.1 to 1.9
- router: bfloat16 [8, 2, 3584, 8], P('pipe'), may hold values from -0.09375 to 0.09375
- w_up: bfloat16 [8, 2, 3584, 8192], P('pipe', None, None, 'expert'), may hold values from -0.09375 to 0.09375
- w_down: bfloat16 [8, 2, 8192, 3584], P('pipe', None, 'expert'), may hold values from -0.1875 to 0.1875
Outputs:
- new_down: bfloat16 [8, 1024, 3584], P('pipe', 'expert')
- new_up: bfloat16 [8, 1024, 3584], P('pipe', 'expert')
The draws below stay inside these ranges and needn't reach their ends.
Inputs may be any that keep to these rules, and one draw needn't show every extreme that they name: `routes`: each row names 2 different experts. Among the 16 tokens of one index of expert (aligned blocks) for one step, pipe index and side, no expert is named by more than 8 tokens, a bound that some block reaches.
All inputs are finite; a program needn't handle non-finite values.
Results may differ from the reference program's by a relative error of at most 0.009.
Values may be sent and summed in bfloat16 or wider, within the bound.
A program may use at most 64 MiB of HBM per device.

```python
import math
import jax
import jax.numpy as jnp
import numpy as np
from jax import lax

D = 3584
EFF = 1024
SPLIT = 8
TOPK = 2
TOK_DEV = 16
STEPS = 1
EXPERTS = 8
TOKENS = 1024
CAP = 8
N_PIPE = 8
N_EXPERT = 64


def steps_of(stream_key, shape, cuts, smallest, largest):
    level, own = 1.0, jax.random.fold_in(stream_key, 6)
    for position, blocks in cuts:
        heights = jnp.exp(jax.random.uniform(jax.random.fold_in(own, position), (blocks,), jnp.float32, smallest / len(cuts), largest / len(cuts)))
        level = level * jnp.repeat(heights, shape[position] // blocks).reshape([-1 if axis == position else 1 for axis in range(len(shape))])
    return level


def routed_block(stream_key, own, number, rows, count, top, limit, lean):
    ranking = jax.random.permutation(stream_key, count)
    packed, common = portions_of(count, rows * top, limit, lean, True), portions_of(count, rows * top, limit, lean, False)
    places = jnp.arange(count)

    def named(sizes, turn):
        used = int((sizes > 0).sum())
        fixed = max(1, used // 4)
        moved = fixed + (places - fixed + turn * (used - fixed)) % max(1, count - fixed)
        return jnp.zeros((count,), jnp.int32).at[ranking[jnp.where(places < fixed, places, moved)]].set(jnp.asarray(sizes, jnp.int32))

    sizes = jnp.where(number % 4 == 0, named(packed, number // 4), named(common, number - number // 4 - 1))
    mixed = jax.random.permutation(jax.random.fold_in(own, 3), count)
    source_of, receiver = mixed[0:count // 2 * 2:2], mixed[1:count // 2 * 2:2]
    slack = jnp.minimum(sizes[source_of] - 1, limit - sizes[receiver]) // 2
    slack = jnp.where((source_of == ranking[0]) | (receiver == ranking[0]) | (sizes[receiver] == 0), 0, jnp.maximum(slack, 0))
    moved = jax.random.randint(jax.random.fold_in(own, 4), (count // 2,), 0, 1 << 20) % (slack + 1)
    sizes = sizes.at[source_of].add(-moved).at[receiver].add(moved)
    members = jnp.searchsorted(jnp.cumsum(sizes), jnp.arange(rows * top), side="right").astype(jnp.int32)
    table = members.reshape(top, rows).T
    table = table[jax.random.permutation(jax.random.fold_in(own, 1), rows)]
    turn = jax.random.randint(jax.random.fold_in(own, 2), (rows, 1), 0, top)
    return jnp.take_along_axis(table, (jnp.arange(top)[None, :] + turn) % top, axis=1)


def portions_of(count, total, bound, skew, full):
    loads = [(1 << 20) // math.isqrt(rank ** skew) + 1 for rank in range(1, count + 1)]
    largest = bound if full else min(bound, max(-(-total // count), total * loads[0] // sum(loads)))
    least = 1 if total - largest >= count - 1 else 0
    given, spare = [largest] + [least] * (count - 1), total - largest - least * (count - 1)
    while spare > 0:
        movable = [i for i in range(1, count) if given[i] < largest] or [i for i in range(1, count) if given[i] < bound]
        whole, remaining = sum([loads[i] for i in movable]), spare
        for i in movable:
            addition = min(bound - given[i], max(1, remaining * loads[i] // whole), spare)
            given[i] = given[i] + addition
            spare = spare - addition
    return np.array(given)


def bell_draw(rng, extent, deviation, limit, cuts=(), kind=jnp.bfloat16):
    drawn = jax.random.normal(rng, extent, jnp.float32) * deviation
    if len(cuts) > 0:
        drawn = steps_of(rng, extent, cuts, -0.22, 0.18) * drawn
    return jnp.clip(drawn, min=-limit, max=limit).astype(kind)


def setup_inputs(seed: int = 0) -> dict:
    seeds = jax.random.split(jax.random.key(seed), 8)
    state_down = bell_draw(seeds[0], (N_PIPE, TOKENS, D), 1.0, 6.0, ((0, 8), (1, 64)))
    state_up = bell_draw(seeds[1], (N_PIPE, TOKENS, D), 1.0, 6.0, ((0, 8), (1, 64)))
    routes_keys = jax.random.split(jax.random.fold_in(seeds[2], 1), STEPS * N_PIPE * 2 * TOKENS // TOK_DEV)
    routes_turns = jax.random.permutation(jax.random.fold_in(seeds[2], 3), STEPS * N_PIPE * 2 * TOKENS // TOK_DEV)
    routes = jax.vmap(lambda own, number: routed_block(jax.random.fold_in(seeds[2], 2), own, number, TOK_DEV, EXPERTS, TOPK, CAP, 2))(routes_keys, routes_turns).reshape((STEPS, N_PIPE, 2, TOKENS, TOPK))
    gains = jnp.clip(1.0 + 0.18 * jax.random.normal(seeds[3], (N_PIPE, 2, D), jnp.float32), 0.1, 1.9)
    router = bell_draw(seeds[4], (N_PIPE, 2, D, EXPERTS), D ** -0.5, 0.09375, ((0, 8),))
    w_up = bell_draw(seeds[5], (N_PIPE, 2, D, EXPERTS * EFF), D ** -0.5, 0.09375, ((0, 8), (3, 64)))
    w_down = bell_draw(seeds[6], (N_PIPE, 2, EXPERTS * EFF, D), EFF ** -0.5, 0.1875, ((0, 8), (2, 64)))
    return {"state_down": state_down, "state_up": state_up, "routes": routes, "gains": gains, "router": router, "w_up": w_up, "w_down": w_down}


epsilon = 1e-06
route_scale = 2.5

def slot_table(block_routes):
    flat_routes = block_routes.reshape(-1)
    expert_hit = (flat_routes[:, None] == jnp.arange(EXPERTS, dtype=jnp.int32)[None, :]).astype(jnp.int32)
    earlier = jnp.cumsum(expert_hit, axis=0) - expert_hit
    slot_index = lax.optimization_barrier(jnp.sum(earlier * expert_hit, axis=1))
    slot_hit = (slot_index[:, None] == jnp.arange(CAP, dtype=jnp.int32)[None, :]).astype(jnp.int32)
    return (expert_hit[:, :, None] * slot_hit[:, None, :]).astype(jnp.float32)

def section_apply(tokens, token_routes, gain_row, router, w_up, w_down):
    wide_tokens = tokens.astype(jnp.float32)
    scale_rows = lax.rsqrt(lax.optimization_barrier(jnp.mean(wide_tokens * wide_tokens, axis=-1, keepdims=True)) + epsilon)
    normed = (wide_tokens * scale_rows * gain_row).astype(jnp.bfloat16)
    logits = jnp.dot(normed, router, preferred_element_type=jnp.float32)
    expert_hit = (token_routes[:, :, None] == jnp.arange(EXPERTS, dtype=jnp.int32)[None, None, :]).astype(jnp.float32)
    affinity = jax.nn.sigmoid(lax.optimization_barrier(jnp.sum(expert_hit * logits[:, None, :], axis=-1)))
    weight = route_scale * affinity / lax.optimization_barrier(jnp.sum(affinity, axis=-1, keepdims=True))
    tables = jax.vmap(slot_table)(token_routes.reshape(N_EXPERT, TOK_DEV, TOPK))
    row_inputs = jnp.repeat(normed.reshape(N_EXPERT, TOK_DEV, D), TOPK, axis=1).astype(jnp.float32)
    buffers = jnp.einsum('nrec,nrd->necd', tables, row_inputs, precision=lax.Precision.HIGHEST).astype(jnp.bfloat16)
    hidden_dev = EFF // SPLIT

    def run_expert(expert_id):
        inputs = buffers[:, expert_id].reshape(N_EXPERT * CAP, D)
        up_cols = lax.dynamic_slice_in_dim(w_up, expert_id * EFF, EFF, 1)
        down_rows = lax.dynamic_slice_in_dim(w_down, expert_id * EFF, EFF, 0)
        hidden = jax.nn.silu(jnp.dot(inputs, up_cols, preferred_element_type=jnp.float32)).astype(jnp.bfloat16)
        pieces = jnp.einsum('rjh,jhd->rjd', hidden.reshape(N_EXPERT * CAP, SPLIT, hidden_dev).astype(jnp.float32), down_rows.reshape(SPLIT, hidden_dev, D).astype(jnp.float32), precision=lax.Precision.HIGHEST).astype(jnp.bfloat16)
        return lax.optimization_barrier(jnp.sum(pieces.astype(jnp.float32), axis=1)).reshape(N_EXPERT, CAP, D)
    outputs = lax.map(run_expert, jnp.arange(EXPERTS, dtype=jnp.int32))
    combined = jnp.einsum('nrec,encd->nrd', tables, outputs, precision=lax.Precision.HIGHEST)
    combined = combined.reshape(TOKENS, TOPK, D)
    branch_sum = lax.optimization_barrier(jnp.sum(weight[:, :, None] * combined, axis=1))
    return (wide_tokens + branch_sum).astype(jnp.bfloat16)

def reference(state_down, state_up, routes, gains, router, w_up, w_down):
    down_state = state_down
    up_state = state_up
    for step_index in range(STEPS):
        down_out = [section_apply(down_state[place], routes[step_index, place, 0], gains[place, 0], router[place, 0], w_up[place, 0], w_down[place, 0]) for place in range(N_PIPE)]
        up_out = [section_apply(up_state[place], routes[step_index, place, 1], gains[place, 1], router[place, 1], w_up[place, 1], w_down[place, 1]) for place in range(N_PIPE)]
        down_state = jnp.stack([up_out[0]] + down_out[:-1])
        up_state = jnp.stack(up_out[1:] + [down_out[-1]])
    return (down_state, up_state)
```

```python
import functools

import jax
import jax.numpy as jnp
from jax import lax
from jax.experimental import pallas as pl
from jax.experimental.pallas import tpu as pltpu
from jax.sharding import PartitionSpec as P

MESH = pl.DeviceIdType.MESH
EPSILON = 1e-06
ROUTE_SCALE = 2.5

NX, NY, NZ = 4, 8, 8
EXPERTS = 8
TOK = 16
CAP = 8
D = 3584
HALF = D // 2
META = 128
WIDE = D + META
TILE = 256
HID = 128
BLOCKS = NY
OWN = BLOCKS
LAG = 3

F32 = jnp.float32
BF16 = jnp.bfloat16


def dot(a, b):
    return jnp.dot(a, b, preferred_element_type=F32)


def dot_lanes(a, b):
    return lax.dot_general(a, b, (((1,), (1,)), ((), ())), preferred_element_type=F32)


def iota(shape, axis):
    return lax.broadcasted_iota(jnp.int32, shape, axis)


def kernel(
    down_ref, up_ref, routes_ref, gains_ref, router_ref, w_up_ref, w_down_ref,
    out_down, out_up,
    tok, sel, sel2, got, got2, ans, ans2, mate, sum2, back, back2, part, part_in, acc, wu, wd, fin, fin_in,
    own_send, a_send, a_recv, b_send, b_recv, f_send, f_recv, m_send, m_recv, d_send, d_recv,
    e_send, e_recv, w_local, w_send, w_recv, z_send, z_recv,
):
    z = lax.axis_index("pipe")
    place = lax.axis_index("expert")
    x = place // (2 * NY)
    y = lax.rem(place // 2, NY)
    core = lax.rem(place, 2)
    half_of_experts = y // (NY // 2)
    mine = lax.rem(y, 2)
    other = 1 - mine

    def at(dz=0, dx=0, dy=0):
        xx = lax.rem(x + dx + NX, NX)
        yy = lax.rem(y + dy + NY, NY)
        return (lax.rem(z + dz + NZ, NZ), (xx * NY + yy) * 2 + core)

    sibling = (z, place + 1 - 2 * core)
    pair = (z, place + 2 - 4 * mine)
    right, left = at(dy=1), at(dy=-1)

    def index_of(offset, parity):
        o = lax.rem(offset + parity + 2 * NY, NY)
        return jnp.where(o == 0, 0, jnp.where(o <= NY // 2, 2 * o - 1, 2 * (NY - o)))

    def index_at(position):
        return position + mine * (1 - 2 * lax.rem(position, 2))

    def offset_at(position):
        ahead = lax.rem(position + mine, 2)
        return (2 * ahead - 1) * ((position + 1) // 2)

    barrier = pltpu.get_barrier_semaphore()
    friends = (right, left, at(dx=1), at(dx=-1), at(dx=2), sibling, at(dz=1), at(dz=-1))
    for friend in friends:
        pl.semaphore_signal(barrier, inc=1, device_id=friend, device_id_type=MESH)

    def remote(src, dst, send, recv, device):
        return pltpu.make_async_remote_copy(
            src_ref=src, dst_ref=dst, send_sem=send, recv_sem=recv, device_id=device, device_id_type=MESH
        )

    def weight_views(index):
        side = index // 2
        if index % 2 == 0:
            return w_up_ref.at[0, side], [wu.at[:, pl.ds((2 * side + o) * HID, HID)] for o in (0, 1)]
        return w_down_ref.at[0, side], [wd.at[pl.ds((2 * side + o) * HID, HID), :] for o in (0, 1)]

    def weight_local(index):
        src, views = weight_views(index)
        return pltpu.make_async_copy(src, views[0], w_local.at[index])

    def weight_remote(index):
        src, views = weight_views(index)
        return remote(src, views[1], w_send.at[index], w_recv.at[index], sibling)

    for index in range(4):
        weight_local(index).start()

    expert_lane = iota((TOK, EXPERTS), 1)
    earlier = (iota((TOK, TOK), 1) < iota((TOK, TOK), 0)).astype(BF16)

    def put(first):
        return (iota((EXPERTS, META), 1) == iota((EXPERTS, META), 0) + first).astype(BF16)

    for side, state_ref in enumerate((down_ref, up_ref)):
        wide = state_ref[0].astype(F32)
        scale_rows = lax.rsqrt(jnp.mean(wide * wide, axis=-1, keepdims=True) + EPSILON)
        normed = (wide * scale_rows * gains_ref[0, side : side + 1, :]).astype(BF16)
        tok[mine, side, :, 0:D] = normed
        logits = dot_lanes(normed, router_ref[side])
        picked = routes_ref[side]
        hit = (picked[:, 0:1] == expert_lane) | (picked[:, 1:2] == expert_lane)
        affinity = jnp.where(hit, jax.nn.sigmoid(logits), 0.0)
        weight = ROUTE_SCALE * affinity / jnp.sum(affinity, axis=-1, keepdims=True)
        slot = dot(earlier, hit.astype(F32).astype(BF16))
        code = jnp.where(hit, slot, -1.0).astype(BF16)
        high = weight.astype(BF16)
        low = (weight - high.astype(F32)).astype(BF16)
        info = dot(code, put(0)) + dot(high, put(EXPERTS)) + dot(low, put(2 * EXPERTS))
        tok[mine, side, :, D:WIDE] = info.astype(BF16)

    pl.semaphore_wait(barrier, len(friends))

    def own_copy(way, side):
        into = index_of(1 - 2 * way, other)
        return remote(
            tok.at[mine, side], tok.at[into, side], own_send.at[way, side], a_recv.at[into, side],
            right if way else left,
        )

    for side in range(2):
        for way in range(2):
            own_copy(way, side).start()
    for index in range(4):
        weight_remote(index).start()

    zeros_half = jnp.zeros((TOK, HALF), BF16)
    for block in range(BLOCKS):
        back2[block, other] = zeros_half

    rows = 4 * TOK
    row = iota((rows, META), 0)
    expert_of_row = 2 * lax.rem(x + lax.shift_right_logical(row, 4), NX) + half_of_experts
    lane = iota((rows, META), 1)

    def spread(first):
        return (lane == expert_of_row + first).astype(BF16)

    def a_passed(position, side):
        ahead = lax.rem(position + mine, 2)
        last = 2 + (ahead if side else 1 - ahead)
        return (position >= 1) & ((position + 1) // 2 <= last)

    def a_copy(position, side):
        block, offset = index_at(position), offset_at(position)
        way = 1 - 2 * lax.rem(position + mine, 2)
        into = index_of(offset - way, other)
        return remote(
            tok.at[block, side], tok.at[into, side], a_send.at[block, side], a_recv.at[into, side], at(dy=way)
        )

    def a_wait(block, side):
        remote(
            tok.at[block, side], tok.at[block, side], a_send.at[block, side], a_recv.at[block, side], right
        ).wait_recv()

    def b_copy(block, kind):
        if kind == 2:
            src, dst = sel2.at[block, mine], got2.at[block, mine]
        else:
            src, dst = sel.at[block, kind], got.at[block, 1 + kind]
        return remote(src, dst, b_send.at[block, kind], b_recv.at[block, kind], at(dx=(1, -1, 2)[kind]))

    def f_copy(block):
        return remote(got2.at[block, mine], got2.at[block, mine], f_send.at[block], f_recv.at[block], pair)

    def f_wait(block):
        remote(
            got2.at[block, other], got2.at[block, other], f_send.at[block], f_recv.at[block], pair
        ).wait_recv()

    def m_copy(block):
        return remote(ans2.at[block, other], mate.at[block], m_send.at[block], m_recv.at[block], pair)

    def d_copy(block, kind):
        if kind == 2:
            src, dst = sum2.at[block], back2.at[block, mine]
        else:
            src, dst = ans.at[block, kind], back.at[block, 1 + kind]
        return remote(src, dst, d_send.at[block, kind], d_recv.at[block, kind], at(dx=(-1, 1, 2)[kind]))

    def choose(block):
        info = tok[block, :, :, D:WIDE].reshape(2 * TOK, META)
        code = dot_lanes(spread(0), info)
        r = iota((rows, 2 * TOK), 0)
        c = iota((rows, 2 * TOK), 1)
        hit = (code == (r & 7).astype(F32)) & ((lax.shift_right_logical(r, 3) & 1) == lax.shift_right_logical(c, 4))
        table = hit.astype(F32).astype(BF16)
        for first in range(0, D, TILE):
            span = slice(first, first + TILE)
            picked = dot(table, tok[block, :, :, span].reshape(2 * TOK, TILE)).astype(BF16)
            got[block, 0, :, span] = picked[0:TOK]
            sel[block, 0, :, span] = picked[TOK : 2 * TOK]
            inner = first % HALF
            sel2[block, first // HALF, :, inner : inner + TILE] = picked[2 * TOK : 3 * TOK]
            sel[block, 1, :, span] = picked[3 * TOK :]

    def experts(block):
        total = jnp.zeros((rows, 4 * HID), F32)
        for part_index in range(2):
            span = slice(part_index * HALF, (part_index + 1) * HALF)
            lhs = jnp.concatenate(
                [got[block, 0, :, span], got[block, 1, :, span], got2[block, part_index], got[block, 2, :, span]], axis=0
            )
            total = total + dot(lhs, wu[span, :])
        hidden = total * jax.nn.sigmoid(total)
        r = iota((rows, 4 * HID), 0)
        c = iota((rows, 4 * HID), 1)
        own_side = (lax.shift_right_logical(r, 3) & 1) == lax.shift_right_logical(c, 8)
        hidden = jnp.where(own_side, hidden, 0.0).astype(BF16)
        for first in range(0, D, TILE):
            span = slice(first, first + TILE)
            result = dot(hidden, wd[:, span]).astype(BF16)
            back[block, 0, :, span] = result[0:TOK]
            ans[block, 0, :, span] = result[TOK : 2 * TOK]
            inner = first % HALF
            ans2[block, first // HALF, :, inner : inner + TILE] = result[2 * TOK : 3 * TOK]
            ans[block, 1, :, span] = result[3 * TOK :]

    def d_start(block):
        d_copy(block, 0).start()
        d_copy(block, 1).start()
        m_copy(block).wait_recv()
        sum2[block] = (ans2[block, mine].astype(F32) + mate[block].astype(F32)).astype(BF16)
        d_copy(block, 2).start()

    def forward_step(step, carry):
        @pl.when(step < BLOCKS)
        def _():
            block = index_at(step)

            @pl.when(step >= 1)
            def _():
                for side in range(2):
                    a_wait(block, side)

                    @pl.when(a_passed(step, side))
                    def _():
                        a_copy(step, side).start()

            choose(block)
            for kind in (2, 0, 1):
                b_copy(block, kind).start()

        @pl.when((step >= 1) & (step <= BLOCKS))
        def _():
            block = index_at(step - 1)
            b_copy(block, 2).wait_recv()
            f_copy(block).start()

        @pl.when(step >= LAG)
        def _():
            block = index_at(step - LAG)

            @pl.when(step == LAG)
            def _():
                for index in range(4):
                    weight_local(index).wait()
                    weight_remote(index).wait_recv()

            b_copy(block, 0).wait_recv()
            b_copy(block, 1).wait_recv()
            f_wait(block)
            experts(block)
            m_copy(block).start()

        @pl.when(step == BLOCKS + 1)
        def _():
            d_start(mine)

        return carry

    lax.fori_loop(0, BLOCKS + LAG, forward_step, 0)

    def combine(block):
        for kind in range(3):
            d_copy(block, kind).wait_recv()
        info = tok[block, :, :, D:WIDE].reshape(2 * TOK, META)
        code = dot_lanes(info, spread(0))
        r = iota((2 * TOK, rows), 0)
        c = iota((2 * TOK, rows), 1)
        hit = (code == (c & 7).astype(F32)) & ((lax.shift_right_logical(c, 3) & 1) == lax.shift_right_logical(r, 4))
        high = jnp.where(hit, dot_lanes(info, spread(EXPERTS)), 0.0).astype(BF16)
        low = jnp.where(hit, dot_lanes(info, spread(2 * EXPERTS)), 0.0).astype(BF16)
        for first in range(0, D, TILE):
            span = slice(first, first + TILE)
            inner = first % HALF
            answers = jnp.concatenate(
                [
                    back[block, 0, :, span],
                    back[block, 1, :, span],
                    back2[block, first // HALF, :, inner : inner + TILE],
                    back[block, 2, :, span],
                ],
                axis=0,
            )
            total = dot(high, answers) + dot(low, answers)
            acc[0, :, span] = total[0:TOK]
            acc[1, :, span] = total[TOK:]

    def e_copy(position, side):
        block, offset = index_at(position), offset_at(position)
        ahead = lax.rem(position + mine, 2)
        ahead = jnp.where(position == BLOCKS - 1, 1 - side, ahead)
        way = 2 * ahead - 1
        into = jnp.where((position + 1) // 2 == 1, OWN + 1 - ahead, index_of(offset - way, other))
        return remote(
            part.at[block, side], part_in.at[into, side], e_send.at[block, side], e_recv.at[into, side], at(dy=way)
        )

    def e_wait(index, side):
        remote(
            part_in.at[index, side], part_in.at[index, side], e_send.at[0, side], e_recv.at[index, side], right
        ).wait_recv()

    d_start(index_at(BLOCKS - 1))
    d_start(index_at(BLOCKS - 2))

    def backward_step(step, carry):
        position = BLOCKS - 1 - step
        block = index_at(position)
        distance = (position + 1) // 2
        ahead = lax.rem(position + mine, 2)

        @pl.when(position >= 3)
        def _():
            d_start(index_at(position - 2))

        combine(block)
        for side in range(2):
            joined = (distance <= 2) | ((distance == 3) & (ahead == 1 - side))

            @pl.when(joined)
            def _():
                e_wait(block, side)
                part[block, side] = (acc[side] + part_in[block, side].astype(F32)).astype(BF16)

            @pl.when(jnp.logical_not(joined))
            def _():
                part[block, side] = acc[side].astype(BF16)

            e_copy(position, side).start()
        return carry

    lax.fori_loop(0, BLOCKS - 1, backward_step, 0)

    combine(mine)
    first_z, last_z = z == 0, z == NZ - 1

    def z_copy(side):
        return remote(
            fin.at[side], fin_in.at[side], z_send.at[side], z_recv.at[side], at(dz=1 - 2 * side)
        )

    for side, state_ref in enumerate((down_ref, up_ref)):
        e_wait(OWN, side)
        e_wait(OWN + 1, side)
        branch = acc[side] + part_in[OWN, side].astype(F32) + part_in[OWN + 1, side].astype(F32)
        fin[side] = (state_ref[0].astype(F32) + branch).astype(BF16)

        @pl.when(jnp.logical_not(last_z if side == 0 else first_z))
        def _():
            z_copy(side).start()

    @pl.when(first_z)
    def _():
        out_down[0] = fin[1]

    @pl.when(last_z)
    def _():
        out_up[0] = fin[0]

    @pl.when(jnp.logical_not(first_z))
    def _():
        z_copy(0).wait_recv()
        out_down[0] = fin_in[0]

    @pl.when(jnp.logical_not(last_z))
    def _():
        z_copy(1).wait_recv()
        out_up[0] = fin_in[1]

    for side in range(2):
        for way in range(2):
            own_copy(way, side).wait_send()

        @pl.when(jnp.logical_not(last_z if side == 0 else first_z))
        def _():
            z_copy(side).wait_send()

    for index in range(4):
        weight_remote(index).wait_send()

    def drain(position, carry):
        block = index_at(position)
        for kind in range(3):
            b_copy(block, kind).wait_send()
            d_copy(block, kind).wait_send()
        f_copy(block).wait_send()
        m_copy(block).wait_send()
        for side in range(2):

            @pl.when(a_passed(position, side))
            def _():
                a_copy(position, side).wait_send()

            @pl.when(position >= 1)
            def _():
                e_copy(position, side).wait_send()

        return carry

    lax.fori_loop(0, BLOCKS, drain, 0)


def on_device(state_down, state_up, routes, gains, router, w_up, w_down):
    vmem = pl.BlockSpec(memory_space=pltpu.VMEM)
    hbm = pl.BlockSpec(memory_space=pl.ANY)
    dma = pltpu.SemaphoreType.DMA
    return pl.pallas_call(
        kernel,
        out_shape=(
            jax.ShapeDtypeStruct(state_down.shape, BF16),
            jax.ShapeDtypeStruct(state_up.shape, BF16),
        ),
        in_specs=[vmem] * 5 + [hbm] * 2,
        out_specs=(vmem, vmem),
        scratch_shapes=[
            pltpu.VMEM((BLOCKS, 2, TOK, WIDE), BF16),
            pltpu.VMEM((BLOCKS, 2, TOK, D), BF16),
            pltpu.VMEM((BLOCKS, 2, TOK, HALF), BF16),
            pltpu.VMEM((BLOCKS, 3, TOK, D), BF16),
            pltpu.VMEM((BLOCKS, 2, TOK, HALF), BF16),
            pltpu.VMEM((BLOCKS, 2, TOK, D), BF16),
            pltpu.VMEM((BLOCKS, 2, TOK, HALF), BF16),
            pltpu.VMEM((BLOCKS, TOK, HALF), BF16),
            pltpu.VMEM((BLOCKS, TOK, HALF), BF16),
            pltpu.VMEM((BLOCKS, 3, TOK, D), BF16),
            pltpu.VMEM((BLOCKS, 2, TOK, HALF), BF16),
            pltpu.VMEM((BLOCKS, 2, TOK, D), BF16),
            pltpu.VMEM((BLOCKS + 2, 2, TOK, D), BF16),
            pltpu.VMEM((2, TOK, D), F32),
            pltpu.VMEM((D, 4 * HID), BF16),
            pltpu.VMEM((4 * HID, D), BF16),
            pltpu.VMEM((2, TOK, D), BF16),
            pltpu.VMEM((2, TOK, D), BF16),
            dma((2, 2)),
            dma((BLOCKS, 2)),
            dma((BLOCKS, 2)),
            dma((BLOCKS, 3)),
            dma((BLOCKS, 3)),
            dma((BLOCKS,)),
            dma((BLOCKS,)),
            dma((BLOCKS,)),
            dma((BLOCKS,)),
            dma((BLOCKS, 3)),
            dma((BLOCKS, 3)),
            dma((BLOCKS, 2)),
            dma((BLOCKS + 2, 2)),
            dma((4,)),
            dma((4,)),
            dma((4,)),
            dma((2,)),
            dma((2,)),
        ],
        compiler_params=pltpu.CompilerParams(
            collective_id=0, has_side_effects=True, vmem_limit_bytes=56 * 2**20
        ),
        name="routed_experts",
    )(state_down, state_up, routes[0, 0], gains, jnp.swapaxes(router[0], 1, 2), w_up, w_down)


def solution(mesh):
    in_specs = (
        P("pipe", "expert", None),
        P("pipe", "expert", None),
        P(None, "pipe", None, "expert", None),
        P("pipe", None, None),
        P("pipe", None, None, None),
        P("pipe", None, None, "expert"),
        P("pipe", None, "expert", None),
    )
    out_specs = (P("pipe", "expert", None), P("pipe", "expert", None))
    return jax.shard_map(
        on_device, mesh=mesh, in_specs=in_specs, out_specs=out_specs, check_vma=False
    )
```

```python
import functools

import jax
import jax.numpy as jnp
from jax import lax
from jax.experimental import pallas as pl
from jax.experimental.pallas import tpu as pltpu
from jax.sharding import PartitionSpec as P

MESH = pl.DeviceIdType.MESH
EPSILON = 1e-06
ROUTE_SCALE = 2.5

NX, NY, NZ = 4, 8, 8
EXPERTS = 8
TOK = 16
CAP = 8
D = 3584
HALF = D // 2
META = 128
WIDE = HALF + META
TILE = 256
HID = 128
BLOCKS = NY
OWN = BLOCKS
LAG_PASS = 2
LAG = 5
FILLER = 3

F32 = jnp.float32
BF16 = jnp.bfloat16


def dot(a, b):
    return jnp.dot(a, b, preferred_element_type=F32)


def dot_lanes(a, b):
    return lax.dot_general(a, b, (((1,), (1,)), ((), ())), preferred_element_type=F32)


def iota(shape, axis):
    return lax.broadcasted_iota(jnp.int32, shape, axis)


def kernel(
    down_ref, up_ref, routes_ref, gains_ref, router_ref, w_up_ref, w_down_ref,
    out_down, out_up,
    tok, sel, sel2, got, got2, ans, ans2, mate, sum2, back, back2, part, part_in, acc, wu, wd, fin, fin_in,
    own_send, a_send, a_recv, b_send, b_recv, f_send, f_recv, m_send, m_recv, d_send, d_recv,
    e_send, e_recv, w_local, w_send, w_recv, z_send, z_recv,
):
    z = lax.axis_index("pipe")
    place = lax.axis_index("expert")
    x = place // (2 * NY)
    y = lax.rem(place // 2, NY)
    core = lax.rem(place, 2)
    half_of_experts = y // (NY // 2)
    mine = lax.rem(y, 2)
    other = 1 - mine

    def at(dz=0, dx=0, dy=0):
        xx = lax.rem(x + dx + NX, NX)
        yy = lax.rem(y + dy + NY, NY)
        return (lax.rem(z + dz + NZ, NZ), (xx * NY + yy) * 2 + core)

    sibling = (z, place + 1 - 2 * core)
    pair = (z, place + 2 - 4 * mine)
    right, left = at(dy=1), at(dy=-1)

    def index_of(offset, parity):
        o = lax.rem(offset + parity + 2 * NY, NY)
        return jnp.where(o == 0, 0, jnp.where(o <= NY // 2, 2 * o - 1, 2 * (NY - o)))

    def index_at(position):
        return position + mine * (1 - 2 * lax.rem(position, 2))

    def offset_at(position):
        ahead = lax.rem(position + mine, 2)
        return (2 * ahead - 1) * ((position + 1) // 2)

    barrier = pltpu.get_barrier_semaphore()
    friends = (right, left, at(dx=1), at(dx=-1), at(dx=2), sibling, at(dz=1), at(dz=-1))
    for friend in friends:
        pl.semaphore_signal(barrier, inc=1, device_id=friend, device_id_type=MESH)

    def remote(src, dst, send, recv, device):
        return pltpu.make_async_remote_copy(
            src_ref=src, dst_ref=dst, send_sem=send, recv_sem=recv, device_id=device, device_id_type=MESH
        )

    def weight_views(index):
        side = index // 2
        if index % 2 == 0:
            return w_up_ref.at[0, side], [wu.at[:, pl.ds((2 * side + o) * HID, HID)] for o in (0, 1)]
        return w_down_ref.at[0, side], [wd.at[pl.ds((2 * side + o) * HID, HID), :] for o in (0, 1)]

    def weight_local(index):
        src, views = weight_views(index)
        return pltpu.make_async_copy(src, views[0], w_local.at[index])

    def weight_remote(index):
        src, views = weight_views(index)
        return remote(src, views[1], w_send.at[index], w_recv.at[index], sibling)

    for index in range(4):
        weight_local(index).start()

    eye = (iota((TOK, TOK), 1) == iota((TOK, TOK), 0)).astype(BF16)
    earlier = (iota((TOK, TOK), 1) < iota((TOK, TOK), 0)).astype(BF16)

    def put(first):
        return (iota((EXPERTS, META), 1) == iota((EXPERTS, META), 0) + first).astype(BF16)

    for side, state_ref in enumerate((down_ref, up_ref)):
        wide = state_ref[0].astype(F32)
        scale_rows = lax.rsqrt(jnp.mean(wide * wide, axis=-1, keepdims=True) + EPSILON)
        normed = (wide * scale_rows * gains_ref[0, side : side + 1, :]).astype(BF16)
        own_rows = slice(side * TOK, (side + 1) * TOK)
        for half in range(2):
            tok[mine, half, own_rows, 0:HALF] = normed[:, half * HALF : (half + 1) * HALF]
        logits = dot_lanes(normed, router_ref[side])
        picked = routes_ref[side]
        named = iota((EXPERTS, TOK), 0)
        hit_rows = ((picked[0:1, :] == named) | (picked[1:2, :] == named)).astype(F32).astype(BF16)
        hit = dot_lanes(eye, hit_rows)
        slot = dot_lanes(earlier, hit_rows)
        affinity = hit * jax.nn.sigmoid(logits)
        weight = ROUTE_SCALE * affinity / jnp.sum(affinity, axis=-1, keepdims=True)
        code = jnp.where(hit > 0.5, slot, -1.0).astype(BF16)
        high = weight.astype(BF16)
        low = (weight - high.astype(F32)).astype(BF16)
        info = dot(code, put(0)) + dot(high, put(EXPERTS)) + dot(low, put(2 * EXPERTS))
        tok[mine, 0, own_rows, HALF:WIDE] = info.astype(BF16)

    pl.semaphore_wait(barrier, len(friends))

    def tok_at(block, half):
        return tok.at[block, half] if half == 0 else tok.at[block, half, :, 0:HALF]

    def own_copy(way, half):
        into = index_of(1 - 2 * way, other)
        return remote(
            tok_at(mine, half), tok_at(into, half), own_send.at[way, half], a_recv.at[into, half],
            right if way else left,
        )

    for half in range(2):
        for way in range(2):
            own_copy(way, half).start()
    for index in range(4):
        weight_remote(index).start()

    zeros_half = jnp.zeros((TOK, HALF), BF16)
    for block in range(BLOCKS):
        back2[block, other] = zeros_half

    rows = 4 * TOK
    row = iota((rows, META), 0)
    expert_of_row = 2 * lax.rem(x + lax.shift_right_logical(row, 4), NX) + half_of_experts
    lane = iota((rows, META), 1)

    def spread(first):
        return (lane == expert_of_row + first).astype(BF16)

    def a_passed(position, half):
        ahead = lax.rem(position + mine, 2)
        last = 2 + (ahead if half else 1 - ahead)
        return (position >= 1) & ((position + 1) // 2 <= last)

    def a_copy(position, half):
        block, offset = index_at(position), offset_at(position)
        way = 1 - 2 * lax.rem(position + mine, 2)
        into = index_of(offset - way, other)
        return remote(
            tok_at(block, half), tok_at(into, half), a_send.at[block, half], a_recv.at[into, half], at(dy=way)
        )

    def a_wait(block, half):
        remote(
            tok_at(block, half), tok_at(block, half), a_send.at[block, half], a_recv.at[block, half], right
        ).wait_recv()

    def b_copy(block, kind, half=0):
        if kind == 2:
            src, dst, number = sel2.at[block, mine], got2.at[block, mine], 4
        else:
            src, dst, number = sel.at[block, kind, half], got.at[block, 1 + kind, half], 2 * kind + half
        return remote(src, dst, b_send.at[block, number], b_recv.at[block, number], at(dx=(1, -1, 2)[kind]))

    def f_copy(block):
        return remote(got2.at[block, mine], got2.at[block, mine], f_send.at[block], f_recv.at[block], pair)

    def f_wait(block):
        remote(
            got2.at[block, other], got2.at[block, other], f_send.at[block], f_recv.at[block], pair
        ).wait_recv()

    def m_copy(block):
        return remote(ans2.at[block, other], mate.at[block], m_send.at[block], m_recv.at[block], pair)

    def d_copy(block, kind, half=0):
        if kind == 2:
            src, dst, number = sum2.at[block], back2.at[block, mine], 4
        else:
            src, dst, number = ans.at[block, kind, half], back.at[block, 1 + kind, half], 2 * kind + half
        return remote(src, dst, d_send.at[block, number], d_recv.at[block, number], at(dx=(-1, 1, 2)[kind]))

    def choose(block, half):
        info = tok[block, 0, :, HALF:WIDE]
        code = dot_lanes(spread(0), info)
        r = iota((rows, 2 * TOK), 0)
        c = iota((rows, 2 * TOK), 1)
        hit = (code == (r & 7).astype(F32)) & ((lax.shift_right_logical(r, 3) & 1) == lax.shift_right_logical(c, 4))
        table = hit.astype(F32).astype(BF16)
        for first in range(0, HALF, TILE):
            span = slice(first, first + TILE)
            picked = dot(table, tok[block, half, :, span]).astype(BF16)
            got[block, 0, half, :, span] = picked[0:TOK]
            sel[block, 0, half, :, span] = picked[TOK : 2 * TOK]
            sel2[block, half, :, span] = picked[2 * TOK : 3 * TOK]
            sel[block, 1, half, :, span] = picked[3 * TOK :]

    def experts(block):
        total = jnp.zeros((rows, 4 * HID), F32)
        for half in range(2):
            lhs = jnp.concatenate(
                [got[block, 0, half], got[block, 1, half], got2[block, half], got[block, 2, half]], axis=0
            )
            total = total + dot(lhs, wu[half * HALF : (half + 1) * HALF, :])
        hidden = total * jax.nn.sigmoid(total)
        r = iota((rows, 4 * HID), 0)
        c = iota((rows, 4 * HID), 1)
        own_side = (lax.shift_right_logical(r, 3) & 1) == lax.shift_right_logical(c, 8)
        hidden = jnp.where(own_side, hidden, 0.0).astype(BF16)
        for half in range(2):
            for first in range(0, HALF, TILE):
                span = slice(first, first + TILE)
                result = dot(hidden, wd[:, half * HALF + first : half * HALF + first + TILE]).astype(BF16)
                back[block, 0, half, :, span] = result[0:TOK]
                ans[block, 0, half, :, span] = result[TOK : 2 * TOK]
                ans2[block, half, :, span] = result[2 * TOK : 3 * TOK]
                ans[block, 1, half, :, span] = result[3 * TOK :]

    def d_near(block, half):
        for kind in range(2):
            d_copy(block, kind, half).start()

    def d_far(block):
        m_copy(block).wait_recv()
        sum2[block] = (ans2[block, mine].astype(F32) + mate[block].astype(F32)).astype(BF16)
        d_copy(block, 2).start()

    def d_whole(block):
        d_near(block, 0)
        d_near(block, 1)
        d_far(block)

    def forward_step(step, carry):
        @pl.when(step < BLOCKS)
        def _():
            block = index_at(step)
            for half in range(2):

                @pl.when(step >= 1)
                def _():
                    a_wait(block, half)

                    @pl.when(a_passed(step, half))
                    def _():
                        a_copy(step, half).start()

                choose(block, half)

                @pl.when(mine == half)
                def _():
                    b_copy(block, 2).start()

                for kind in range(2):
                    b_copy(block, kind, half).start()

        @pl.when((step >= LAG_PASS) & (step < BLOCKS + LAG_PASS))
        def _():
            block = index_at(step - LAG_PASS)
            b_copy(block, 2).wait_recv()
            f_copy(block).start()

        @pl.when(step >= LAG)
        def _():
            block = index_at(step - LAG)

            @pl.when(step == LAG)
            def _():
                for index in range(4):
                    weight_local(index).wait()
                    weight_remote(index).wait_recv()

            for half in range(2):
                for kind in range(2):
                    b_copy(block, kind, half).wait_recv()
            f_wait(block)
            experts(block)
            m_copy(block).start()

            @pl.when(step >= BLOCKS + LAG - 2)
            def _():
                d_near(block, 0)
                d_near(block, 1)

        @pl.when(step == BLOCKS)
        def _():
            d_whole(index_at(FILLER))

        return carry

    lax.fori_loop(0, BLOCKS + LAG, forward_step, 0)

    def combine(block, half):
        for kind in range(2):
            d_copy(block, kind, half).wait_recv()

        @pl.when(mine == half)
        def _():
            d_copy(block, 2).wait_recv()

        info = tok[block, 0, :, HALF:WIDE]
        code = dot_lanes(info, spread(0))
        r = iota((2 * TOK, rows), 0)
        c = iota((2 * TOK, rows), 1)
        hit = (code == (c & 7).astype(F32)) & ((lax.shift_right_logical(c, 3) & 1) == lax.shift_right_logical(r, 4))
        high = jnp.where(hit, dot_lanes(info, spread(EXPERTS)), 0.0).astype(BF16)
        low = jnp.where(hit, dot_lanes(info, spread(2 * EXPERTS)), 0.0).astype(BF16)
        for first in range(0, HALF, TILE):
            span = slice(first, first + TILE)
            answers = jnp.concatenate(
                [
                    back[block, 0, half, :, span],
                    back[block, 1, half, :, span],
                    back2[block, half, :, span],
                    back[block, 2, half, :, span],
                ],
                axis=0,
            )
            acc[half, :, span] = dot(high, answers) + dot(low, answers)

    def e_copy(position, half):
        block, offset = index_at(position), offset_at(position)
        ahead = lax.rem(position + mine, 2)
        ahead = jnp.where(position == BLOCKS - 1, 1 - half, ahead)
        way = 2 * ahead - 1
        into = jnp.where((position + 1) // 2 == 1, OWN + 1 - ahead, index_of(offset - way, other))
        return remote(
            part.at[block, half], part_in.at[into, half], e_send.at[block, half], e_recv.at[into, half], at(dy=way)
        )

    def e_wait(index, half):
        remote(
            part_in.at[index, half], part_in.at[index, half], e_send.at[0, half], e_recv.at[index, half], right
        ).wait_recv()

    def join(position, half):
        block = index_at(position)
        distance = (position + 1) // 2
        ahead = lax.rem(position + mine, 2)
        combine(block, half)
        joined = (distance <= 2) | ((distance == 3) & (ahead == 1 - half))

        @pl.when(joined)
        def _():
            e_wait(block, half)
            part[block, half] = (acc[half] + part_in[block, half].astype(F32)).astype(BF16)

        @pl.when(jnp.logical_not(joined))
        def _():
            part[block, half] = acc[half].astype(BF16)

        e_copy(position, half).start()

    d_far(index_at(BLOCKS - 1))
    d_far(index_at(BLOCKS - 2))
    for position in range(BLOCKS - 3, -1, -1):
        if position != FILLER:
            d_whole(index_at(position))
    for half in range(2):
        join(BLOCKS - 1, half)

    def backward_step(step, carry):
        distance = NY // 2 - 1 - step

        for half in range(2):
            join(2 * distance, half)
            join(2 * distance - 1, half)

        return carry

    lax.fori_loop(0, NY // 2 - 1, backward_step, 0)

    first_z, last_z = z == 0, z == NZ - 1

    def z_copy(side, half):
        return remote(
            fin.at[side, half], fin_in.at[side, half], z_send.at[side, half], z_recv.at[side, half],
            at(dz=1 - 2 * side),
        )

    for half in range(2):
        combine(mine, half)
        span = slice(half * HALF, (half + 1) * HALF)
        e_wait(OWN, half)
        e_wait(OWN + 1, half)
        for side, state_ref in enumerate((down_ref, up_ref)):
            own_rows = slice(side * TOK, (side + 1) * TOK)
            branch = acc[half, own_rows] + part_in[OWN, half, own_rows].astype(F32)
            branch = branch + part_in[OWN + 1, half, own_rows].astype(F32)
            fin[side, half] = (state_ref[0, :, span].astype(F32) + branch).astype(BF16)

            @pl.when(jnp.logical_not(last_z if side == 0 else first_z))
            def _():
                z_copy(side, half).start()

    for half in range(2):
        for way in range(2):
            own_copy(way, half).wait_send()

    for index in range(4):
        weight_remote(index).wait_send()

    def drain(position, carry):
        block = index_at(position)
        for half in range(2):
            for kind in range(2):
                b_copy(block, kind, half).wait_send()
                d_copy(block, kind, half).wait_send()

            @pl.when(a_passed(position, half))
            def _():
                a_copy(position, half).wait_send()

            @pl.when(position >= 1)
            def _():
                e_copy(position, half).wait_send()

        b_copy(block, 2).wait_send()
        d_copy(block, 2).wait_send()
        f_copy(block).wait_send()
        m_copy(block).wait_send()
        return carry

    lax.fori_loop(0, BLOCKS, drain, 0)

    for half in range(2):
        span = slice(half * HALF, (half + 1) * HALF)

        @pl.when(first_z)
        def _():
            out_down[0, :, span] = fin[1, half]

        @pl.when(last_z)
        def _():
            out_up[0, :, span] = fin[0, half]

        @pl.when(jnp.logical_not(first_z))
        def _():
            z_copy(0, half).wait_recv()
            out_down[0, :, span] = fin_in[0, half]
            z_copy(1, half).wait_send()

        @pl.when(jnp.logical_not(last_z))
        def _():
            z_copy(1, half).wait_recv()
            out_up[0, :, span] = fin_in[1, half]
            z_copy(0, half).wait_send()


def on_device(state_down, state_up, routes, gains, router, w_up, w_down):
    vmem = pl.BlockSpec(memory_space=pltpu.VMEM)
    hbm = pl.BlockSpec(memory_space=pl.ANY)
    dma = pltpu.SemaphoreType.DMA
    return pl.pallas_call(
        kernel,
        out_shape=(
            jax.ShapeDtypeStruct(state_down.shape, BF16),
            jax.ShapeDtypeStruct(state_up.shape, BF16),
        ),
        in_specs=[vmem] * 5 + [hbm] * 2,
        out_specs=(vmem, vmem),
        scratch_shapes=[
            pltpu.VMEM((BLOCKS, 2, 2 * TOK, WIDE), BF16),
            pltpu.VMEM((BLOCKS, 2, 2, TOK, HALF), BF16),
            pltpu.VMEM((BLOCKS, 2, TOK, HALF), BF16),
            pltpu.VMEM((BLOCKS, 3, 2, TOK, HALF), BF16),
            pltpu.VMEM((BLOCKS, 2, TOK, HALF), BF16),
            pltpu.VMEM((BLOCKS, 2, 2, TOK, HALF), BF16),
            pltpu.VMEM((BLOCKS, 2, TOK, HALF), BF16),
            pltpu.VMEM((BLOCKS, TOK, HALF), BF16),
            pltpu.VMEM((BLOCKS, TOK, HALF), BF16),
            pltpu.VMEM((BLOCKS, 3, 2, TOK, HALF), BF16),
            pltpu.VMEM((BLOCKS, 2, TOK, HALF), BF16),
            pltpu.VMEM((BLOCKS, 2, 2 * TOK, HALF), BF16),
            pltpu.VMEM((BLOCKS + 2, 2, 2 * TOK, HALF), BF16),
            pltpu.VMEM((2, 2 * TOK, HALF), F32),
            pltpu.VMEM((D, 4 * HID), BF16),
            pltpu.VMEM((4 * HID, D), BF16),
            pltpu.VMEM((2, 2, TOK, HALF), BF16),
            pltpu.VMEM((2, 2, TOK, HALF), BF16),
            dma((2, 2)),
            dma((BLOCKS, 2)),
            dma((BLOCKS, 2)),
            dma((BLOCKS, 5)),
            dma((BLOCKS, 5)),
            dma((BLOCKS,)),
            dma((BLOCKS,)),
            dma((BLOCKS,)),
            dma((BLOCKS,)),
            dma((BLOCKS, 5)),
            dma((BLOCKS, 5)),
            dma((BLOCKS, 2)),
            dma((BLOCKS + 2, 2)),
            dma((4,)),
            dma((4,)),
            dma((4,)),
            dma((2, 2)),
            dma((2, 2)),
        ],
        compiler_params=pltpu.CompilerParams(
            collective_id=0, has_side_effects=True, vmem_limit_bytes=56 * 2**20
        ),
        name="routed_experts",
    )(state_down, state_up, jnp.swapaxes(routes[0, 0], 1, 2), gains, jnp.swapaxes(router[0], 1, 2), w_up, w_down)


def solution(mesh):
    in_specs = (
        P("pipe", "expert", None),
        P("pipe", "expert", None),
        P(None, "pipe", None, "expert", None),
        P("pipe", None, None),
        P("pipe", None, None, None),
        P("pipe", None, None, "expert"),
        P("pipe", None, "expert", None),
    )
    out_specs = (P("pipe", "expert", None), P("pipe", "expert", None))
    return jax.shard_map(
        on_device, mesh=mesh, in_specs=in_specs, out_specs=out_specs, check_vma=False
    )
```

```python
import functools

import jax
import jax.numpy as jnp
from jax import lax
from jax.experimental import pallas as pl
from jax.experimental.pallas import tpu as pltpu
from jax.sharding import PartitionSpec as P

MESH = pl.DeviceIdType.MESH
EPSILON = 1e-06
ROUTE_SCALE = 2.5

NX, NY, NZ = 4, 8, 8
EXPERTS = 8
TOK = 16
CAP = 8
D = 3584
HALF = D // 2
META = 128
WIDE = HALF + META
TILE = 256
HID = 128
BLOCKS = NY
LAG_PASS = 2
LAG = 5
FILLER = 3

F32 = jnp.float32
BF16 = jnp.bfloat16


def dot(a, b):
    return jnp.dot(a, b, preferred_element_type=F32)


def dot_lanes(a, b):
    return lax.dot_general(a, b, (((1,), (1,)), ((), ())), preferred_element_type=F32)


def iota(shape, axis):
    return lax.broadcasted_iota(jnp.int32, shape, axis)


def kernel(
    down_ref, up_ref, routes_ref, gains_ref, router_ref, w_up_ref, w_down_ref,
    out_down, out_up,
    tok, sel, sel2, got, got2, ans, ans2, mate, sum2, back, back2, part, part_in, acc, wu, wd, fin, fin_in,
    own_send, a_send, a_recv, b_send, b_recv, f_send, f_recv, m_send, m_recv, d_send, d_recv,
    e_send, e_recv, l_send, w_local, w_send, w_recv, z_send, z_recv,
):
    z = lax.axis_index("pipe")
    place = lax.axis_index("expert")
    x = place // (2 * NY)
    y = lax.rem(place // 2, NY)
    core = lax.rem(place, 2)
    half_of_experts = y // (NY // 2)
    mine = lax.rem(y, 2)
    other = 1 - mine

    def at(dz=0, dx=0, dy=0):
        xx = lax.rem(x + dx + NX, NX)
        yy = lax.rem(y + dy + NY, NY)
        return (lax.rem(z + dz + NZ, NZ), (xx * NY + yy) * 2 + core)

    sibling = (z, place + 1 - 2 * core)
    pair = (z, place + 2 - 4 * mine)
    right, left = at(dy=1), at(dy=-1)

    def index_of(offset, parity):
        o = lax.rem(offset + parity + 2 * NY, NY)
        return jnp.where(o == 0, 0, jnp.where(o <= NY // 2, 2 * o - 1, 2 * (NY - o)))

    def index_at(position):
        return position + mine * (1 - 2 * lax.rem(position, 2))

    def offset_at(position):
        ahead = lax.rem(position + mine, 2)
        return (2 * ahead - 1) * ((position + 1) // 2)

    barrier = pltpu.get_barrier_semaphore()
    friends = (right, left, at(dx=1), at(dx=-1), at(dx=2), sibling)
    friends += tuple(at(dz=dz, dy=dy) for dz in (1, -1) for dy in (0, 1, -1))
    for friend in friends:
        pl.semaphore_signal(barrier, inc=1, device_id=friend, device_id_type=MESH)

    def remote(src, dst, send, recv, device):
        return pltpu.make_async_remote_copy(
            src_ref=src, dst_ref=dst, send_sem=send, recv_sem=recv, device_id=device, device_id_type=MESH
        )

    def weight_views(index):
        side = index // 2
        if index % 2 == 0:
            return w_up_ref.at[0, side], [wu.at[:, pl.ds((2 * side + o) * HID, HID)] for o in (0, 1)]
        return w_down_ref.at[0, side], [wd.at[pl.ds((2 * side + o) * HID, HID), :] for o in (0, 1)]

    def weight_local(index):
        src, views = weight_views(index)
        return pltpu.make_async_copy(src, views[0], w_local.at[index])

    def weight_remote(index):
        src, views = weight_views(index)
        return remote(src, views[1], w_send.at[index], w_recv.at[index], sibling)

    for index in range(4):
        weight_local(index).start()

    eye = (iota((TOK, TOK), 1) == iota((TOK, TOK), 0)).astype(BF16)
    earlier = (iota((TOK, TOK), 1) < iota((TOK, TOK), 0)).astype(BF16)

    def put(first):
        return (iota((EXPERTS, META), 1) == iota((EXPERTS, META), 0) + first).astype(BF16)

    for side, state_ref in enumerate((down_ref, up_ref)):
        wide = state_ref[0].astype(F32)
        scale_rows = lax.rsqrt(jnp.mean(wide * wide, axis=-1, keepdims=True) + EPSILON)
        normed = (wide * scale_rows * gains_ref[0, side : side + 1, :]).astype(BF16)
        own_rows = slice(side * TOK, (side + 1) * TOK)
        for half in range(2):
            tok[mine, half, own_rows, 0:HALF] = normed[:, half * HALF : (half + 1) * HALF]
        logits = dot_lanes(normed, router_ref[side])
        picked = routes_ref[side]
        named = iota((EXPERTS, TOK), 0)
        hit_rows = ((picked[0:1, :] == named) | (picked[1:2, :] == named)).astype(F32).astype(BF16)
        hit = dot_lanes(eye, hit_rows)
        slot = dot_lanes(earlier, hit_rows)
        affinity = hit * jax.nn.sigmoid(logits)
        weight = ROUTE_SCALE * affinity / jnp.sum(affinity, axis=-1, keepdims=True)
        code = jnp.where(hit > 0.5, slot, -1.0).astype(BF16)
        high = weight.astype(BF16)
        low = (weight - high.astype(F32)).astype(BF16)
        info = dot(code, put(0)) + dot(high, put(EXPERTS)) + dot(low, put(2 * EXPERTS))
        tok[mine, 0, own_rows, HALF:WIDE] = info.astype(BF16)

    pl.semaphore_wait(barrier, len(friends))

    def tok_at(block, half):
        return tok.at[block, half] if half == 0 else tok.at[block, half, :, 0:HALF]

    def own_copy(way, half):
        into = index_of(1 - 2 * way, other)
        return remote(
            tok_at(mine, half), tok_at(into, half), own_send.at[way, half], a_recv.at[into, half],
            right if way else left,
        )

    for half in range(2):
        for way in range(2):
            own_copy(way, half).start()
    for index in range(4):
        weight_remote(index).start()

    zeros_half = jnp.zeros((TOK, HALF), BF16)
    for block in range(BLOCKS):
        back2[block, other] = zeros_half

    rows = 4 * TOK
    row = iota((rows, META), 0)
    expert_of_row = 2 * lax.rem(x + lax.shift_right_logical(row, 4), NX) + half_of_experts
    lane = iota((rows, META), 1)

    def spread(first):
        return (lane == expert_of_row + first).astype(BF16)

    def a_passed(position, half):
        ahead = lax.rem(position + mine, 2)
        last = 2 + (ahead if half else 1 - ahead)
        return (position >= 1) & ((position + 1) // 2 <= last)

    def a_copy(position, half):
        block, offset = index_at(position), offset_at(position)
        way = 1 - 2 * lax.rem(position + mine, 2)
        into = index_of(offset - way, other)
        return remote(
            tok_at(block, half), tok_at(into, half), a_send.at[block, half], a_recv.at[into, half], at(dy=way)
        )

    def a_wait(block, half):
        remote(
            tok_at(block, half), tok_at(block, half), a_send.at[block, half], a_recv.at[block, half], right
        ).wait_recv()

    def b_copy(block, kind, half=0):
        if kind == 2:
            src, dst, number = sel2.at[block, mine], got2.at[block, mine], 4
        else:
            src, dst, number = sel.at[block, kind, half], got.at[block, 1 + kind, half], 2 * kind + half
        return remote(src, dst, b_send.at[block, number], b_recv.at[block, number], at(dx=(1, -1, 2)[kind]))

    def f_copy(block):
        return remote(got2.at[block, mine], got2.at[block, mine], f_send.at[block], f_recv.at[block], pair)

    def f_wait(block):
        remote(
            got2.at[block, other], got2.at[block, other], f_send.at[block], f_recv.at[block], pair
        ).wait_recv()

    def m_copy(block):
        return remote(ans2.at[block, other], mate.at[block], m_send.at[block], m_recv.at[block], pair)

    def d_copy(block, kind, half=0):
        if kind == 2:
            src, dst, number = sum2.at[block], back2.at[block, mine], 4
        else:
            src, dst, number = ans.at[block, kind, half], back.at[block, 1 + kind, half], 2 * kind + half
        return remote(src, dst, d_send.at[block, number], d_recv.at[block, number], at(dx=(-1, 1, 2)[kind]))

    def choose(block, half):
        info = tok[block, 0, :, HALF:WIDE]
        code = dot_lanes(spread(0), info)
        r = iota((rows, 2 * TOK), 0)
        c = iota((rows, 2 * TOK), 1)
        hit = (code == (r & 7).astype(F32)) & ((lax.shift_right_logical(r, 3) & 1) == lax.shift_right_logical(c, 4))
        table = hit.astype(F32).astype(BF16)
        for first in range(0, HALF, TILE):
            span = slice(first, first + TILE)
            picked = dot(table, tok[block, half, :, span]).astype(BF16)
            got[block, 0, half, :, span] = picked[0:TOK]
            sel[block, 0, half, :, span] = picked[TOK : 2 * TOK]
            sel2[block, half, :, span] = picked[2 * TOK : 3 * TOK]
            sel[block, 1, half, :, span] = picked[3 * TOK :]

    def experts(block):
        total = jnp.zeros((rows, 4 * HID), F32)
        for half in range(2):
            lhs = jnp.concatenate(
                [got[block, 0, half], got[block, 1, half], got2[block, half], got[block, 2, half]], axis=0
            )
            total = total + dot(lhs, wu[half * HALF : (half + 1) * HALF, :])
        hidden = total * jax.nn.sigmoid(total)
        r = iota((rows, 4 * HID), 0)
        c = iota((rows, 4 * HID), 1)
        own_side = (lax.shift_right_logical(r, 3) & 1) == lax.shift_right_logical(c, 8)
        hidden = jnp.where(own_side, hidden, 0.0).astype(BF16)
        for half in range(2):
            for first in range(0, HALF, TILE):
                span = slice(first, first + TILE)
                result = dot(hidden, wd[:, half * HALF + first : half * HALF + first + TILE]).astype(BF16)
                back[block, 0, half, :, span] = result[0:TOK]
                ans[block, 0, half, :, span] = result[TOK : 2 * TOK]
                ans2[block, half, :, span] = result[2 * TOK : 3 * TOK]
                ans[block, 1, half, :, span] = result[3 * TOK :]

    def d_near(block, half):
        for kind in range(2):
            d_copy(block, kind, half).start()

    def d_far(block):
        m_copy(block).wait_recv()
        sum2[block] = (ans2[block, mine].astype(F32) + mate[block].astype(F32)).astype(BF16)
        d_copy(block, 2).start()

    def d_whole(block):
        d_near(block, 0)
        d_near(block, 1)
        d_far(block)

    def forward_step(step, carry):
        @pl.when(step < BLOCKS)
        def _():
            block = index_at(step)
            for half in range(2):

                @pl.when(step >= 1)
                def _():
                    a_wait(block, half)

                    @pl.when(a_passed(step, half))
                    def _():
                        a_copy(step, half).start()

                choose(block, half)

                @pl.when(mine == half)
                def _():
                    b_copy(block, 2).start()

                for kind in range(2):
                    b_copy(block, kind, half).start()

        @pl.when((step >= LAG_PASS) & (step < BLOCKS + LAG_PASS))
        def _():
            block = index_at(step - LAG_PASS)
            b_copy(block, 2).wait_recv()
            f_copy(block).start()

        @pl.when(step >= LAG)
        def _():
            block = index_at(step - LAG)

            @pl.when(step == LAG)
            def _():
                for index in range(4):
                    weight_local(index).wait()
                    weight_remote(index).wait_recv()

            for half in range(2):
                for kind in range(2):
                    b_copy(block, kind, half).wait_recv()
            f_wait(block)
            experts(block)
            m_copy(block).start()

            @pl.when(step >= BLOCKS + LAG - 2)
            def _():
                d_near(block, 0)
                d_near(block, 1)

        @pl.when(step == BLOCKS)
        def _():
            d_whole(index_at(FILLER))

        return carry

    lax.fori_loop(0, BLOCKS + LAG, forward_step, 0)

    def combine(block, half):
        for kind in range(2):
            d_copy(block, kind, half).wait_recv()

        @pl.when(mine == half)
        def _():
            d_copy(block, 2).wait_recv()

        info = tok[block, 0, :, HALF:WIDE]
        code = dot_lanes(info, spread(0))
        r = iota((2 * TOK, rows), 0)
        c = iota((2 * TOK, rows), 1)
        hit = (code == (c & 7).astype(F32)) & ((lax.shift_right_logical(c, 3) & 1) == lax.shift_right_logical(r, 4))
        high = jnp.where(hit, dot_lanes(info, spread(EXPERTS)), 0.0).astype(BF16)
        low = jnp.where(hit, dot_lanes(info, spread(2 * EXPERTS)), 0.0).astype(BF16)
        for first in range(0, HALF, TILE):
            span = slice(first, first + TILE)
            answers = jnp.concatenate(
                [
                    back[block, 0, half, :, span],
                    back[block, 1, half, :, span],
                    back2[block, half, :, span],
                    back[block, 2, half, :, span],
                ],
                axis=0,
            )
            acc[half, :, span] = dot(high, answers) + dot(low, answers)

    def e_copy(position, half):
        block, offset = index_at(position), offset_at(position)
        ahead = lax.rem(position + mine, 2)
        ahead = jnp.where(position == BLOCKS - 1, 1 - half, ahead)
        way = 2 * ahead - 1
        into = index_of(offset - way, other)
        return remote(
            part.at[block, half], part_in.at[into, half], e_send.at[block, half], e_recv.at[into, half], at(dy=way)
        )

    def e_wait(index, half):
        remote(
            part_in.at[index, half], part_in.at[index, half], e_send.at[0, half], e_recv.at[index, half], right
        ).wait_recv()

    def join(position, half):
        block = index_at(position)
        distance = (position + 1) // 2
        ahead = lax.rem(position + mine, 2)
        combine(block, half)
        joined = (distance <= 2) | ((distance == 3) & (ahead == 1 - half))

        @pl.when(joined)
        def _():
            e_wait(block, half)
            part[block, half] = (acc[half] + part_in[block, half].astype(F32)).astype(BF16)

        @pl.when(jnp.logical_not(joined))
        def _():
            part[block, half] = acc[half].astype(BF16)

    first_z, last_z = z == 0, z == NZ - 1
    stays = (last_z, first_z)
    steps_z = (jnp.where(last_z, 0, 1), jnp.where(first_z, 0, -1))
    results = (jnp.where(last_z, 1, 0), jnp.where(first_z, 0, 1))

    def last_copy(position, half, side):
        block = index_at(position)
        ahead = lax.rem(position + mine, 2)
        result, source = results[side], 2 - ahead
        return remote(
            part.at[block, half, pl.ds(side * TOK, TOK)], fin_in.at[result, source, half],
            l_send.at[position, half, side], z_recv.at[result, source, half],
            at(dz=steps_z[side], dy=2 * ahead - 1),
        )

    def z_copy(side, half):
        return remote(
            fin.at[side, half], fin_in.at[side, 0, half], z_send.at[side, half], z_recv.at[side, 0, half],
            at(dz=1 - 2 * side),
        )

    d_far(index_at(BLOCKS - 1))
    d_far(index_at(BLOCKS - 2))
    for position in range(BLOCKS - 3, -1, -1):
        if position != FILLER:
            d_whole(index_at(position))
    for half in range(2):
        join(BLOCKS - 1, half)
        e_copy(BLOCKS - 1, half).start()

    def backward_step(step, carry):
        distance = NY // 2 - 1 - step

        for half in range(2):
            for position in (2 * distance, 2 * distance - 1):
                join(position, half)
                e_copy(position, half).start()

        return carry

    lax.fori_loop(0, NY // 2 - 2, backward_step, 0)

    for half in range(2):
        for position in (2, 1):
            join(position, half)
            for side in range(2):
                last_copy(position, half, side).start()

    for half in range(2):
        combine(mine, half)
        span = slice(half * HALF, (half + 1) * HALF)
        for side, state_ref in enumerate((down_ref, up_ref)):
            fin[side, half] = (
                state_ref[0, :, span].astype(F32) + acc[half, side * TOK : (side + 1) * TOK]
            ).astype(BF16)

            @pl.when(jnp.logical_not(stays[side]))
            def _():
                z_copy(side, half).start()

            @pl.when(stays[side])
            def _():
                fin_in[1 - side, 0, half] = fin[side, half]

    for half in range(2):
        for way in range(2):
            own_copy(way, half).wait_send()

    for index in range(4):
        weight_remote(index).wait_send()

    def drain(position, carry):
        block = index_at(position)
        for half in range(2):
            for kind in range(2):
                b_copy(block, kind, half).wait_send()
                d_copy(block, kind, half).wait_send()

            @pl.when(a_passed(position, half))
            def _():
                a_copy(position, half).wait_send()

            @pl.when(position >= 3)
            def _():
                e_copy(position, half).wait_send()

        b_copy(block, 2).wait_send()
        d_copy(block, 2).wait_send()
        f_copy(block).wait_send()
        m_copy(block).wait_send()
        return carry

    lax.fori_loop(0, BLOCKS, drain, 0)

    for half in range(2):
        for position in (2, 1):
            for side in range(2):
                last_copy(position, half, side).wait_send()
        span = slice(half * HALF, (half + 1) * HALF)
        for side, out in enumerate((out_down, out_up)):

            @pl.when(jnp.logical_not(stays[side]))
            def _():
                z_copy(side, half).wait_send()

            @pl.when(jnp.logical_not(stays[1 - side]))
            def _():
                z_copy(side, half).wait_recv()

            total = fin_in[side, 0, half].astype(F32)
            for source in (1, 2):
                remote(
                    fin_in.at[side, source, half], fin_in.at[side, source, half],
                    z_send.at[side, half], z_recv.at[side, source, half], right,
                ).wait_recv()
                total = total + fin_in[side, source, half].astype(F32)
            out[0, :, span] = total.astype(BF16)


def on_device(state_down, state_up, routes, gains, router, w_up, w_down):
    vmem = pl.BlockSpec(memory_space=pltpu.VMEM)
    hbm = pl.BlockSpec(memory_space=pl.ANY)
    dma = pltpu.SemaphoreType.DMA
    return pl.pallas_call(
        kernel,
        out_shape=(
            pltpu.VMEM(state_down.shape, BF16),
            pltpu.VMEM(state_up.shape, BF16),
        ),
        in_specs=[vmem] * 5 + [hbm] * 2,
        out_specs=(vmem, vmem),
        scratch_shapes=[
            pltpu.VMEM((BLOCKS, 2, 2 * TOK, WIDE), BF16),
            pltpu.VMEM((BLOCKS, 2, 2, TOK, HALF), BF16),
            pltpu.VMEM((BLOCKS, 2, TOK, HALF), BF16),
            pltpu.VMEM((BLOCKS, 3, 2, TOK, HALF), BF16),
            pltpu.VMEM((BLOCKS, 2, TOK, HALF), BF16),
            pltpu.VMEM((BLOCKS, 2, 2, TOK, HALF), BF16),
            pltpu.VMEM((BLOCKS, 2, TOK, HALF), BF16),
            pltpu.VMEM((BLOCKS, TOK, HALF), BF16),
            pltpu.VMEM((BLOCKS, TOK, HALF), BF16),
            pltpu.VMEM((BLOCKS, 3, 2, TOK, HALF), BF16),
            pltpu.VMEM((BLOCKS, 2, TOK, HALF), BF16),
            pltpu.VMEM((BLOCKS, 2, 2 * TOK, HALF), BF16),
            pltpu.VMEM((BLOCKS, 2, 2 * TOK, HALF), BF16),
            pltpu.VMEM((2, 2 * TOK, HALF), F32),
            pltpu.VMEM((D, 4 * HID), BF16),
            pltpu.VMEM((4 * HID, D), BF16),
            pltpu.VMEM((2, 2, TOK, HALF), BF16),
            pltpu.VMEM((2, 3, 2, TOK, HALF), BF16),
            dma((2, 2)),
            dma((BLOCKS, 2)),
            dma((BLOCKS, 2)),
            dma((BLOCKS, 5)),
            dma((BLOCKS, 5)),
            dma((BLOCKS,)),
            dma((BLOCKS,)),
            dma((BLOCKS,)),
            dma((BLOCKS,)),
            dma((BLOCKS, 5)),
            dma((BLOCKS, 5)),
            dma((BLOCKS, 2)),
            dma((BLOCKS, 2)),
            dma((3, 2, 2)),
            dma((4,)),
            dma((4,)),
            dma((4,)),
            dma((2, 2)),
            dma((2, 3, 2)),
        ],
        compiler_params=pltpu.CompilerParams(
            collective_id=0, has_side_effects=True, vmem_limit_bytes=56 * 2**20
        ),
        name="routed_experts",
    )(state_down, state_up, jnp.swapaxes(routes[0, 0], 1, 2), gains, jnp.swapaxes(router[0], 1, 2), w_up, w_down)


def solution(mesh):
    in_specs = (
        P("pipe", "expert", None),
        P("pipe", "expert", None),
        P(None, "pipe", None, "expert", None),
        P("pipe", None, None),
        P("pipe", None, None, None),
        P("pipe", None, None, "expert"),
        P("pipe", None, "expert", None),
    )
    out_specs = (P("pipe", "expert", None), P("pipe", "expert", None))
    return jax.shard_map(
        on_device, mesh=mesh, in_specs=in_specs, out_specs=out_specs, check_vma=False
    )
```

```python
import functools

import jax
import jax.numpy as jnp
from jax import lax
from jax.experimental import pallas as pl
from jax.experimental.pallas import tpu as pltpu
from jax.sharding import PartitionSpec as P

MESH = pl.DeviceIdType.MESH
EPSILON = 1e-06
ROUTE_SCALE = 2.5

NX, NY, NZ = 4, 8, 8
EXPERTS = 8
TOK = 16
CAP = 8
D = 3584
HALF = D // 2
META = 128
WIDE = HALF + META
TILE = 256
HID = 128
BLOCKS = NY
LAG_PASS = 2
LAG = 5
FILLER = 3

F32 = jnp.float32
BF16 = jnp.bfloat16


def dot(a, b):
    return jnp.dot(a, b, preferred_element_type=F32)


def dot_lanes(a, b):
    return lax.dot_general(a, b, (((1,), (1,)), ((), ())), preferred_element_type=F32)


def iota(shape, axis):
    return lax.broadcasted_iota(jnp.int32, shape, axis)


def kernel(
    down_hbm, up_hbm, routes_hbm, gains_hbm, router_hbm, w_up_ref, w_down_ref,
    out_down, out_up,
    down_ref, up_ref, routes_ref, gains_ref, router_ref, in_local,
    tok, sel, sel2, got, got2, ans, ans2, mate, sum2, back, back2, part, part_in, acc, wu, wd, fin, fin_in,
    own_send, a_send, a_recv, b_send, b_recv, f_send, f_recv, m_send, m_recv, d_send, d_recv,
    e_send, e_recv, l_send, w_local, w_send, w_recv, z_send, z_recv,
):
    z = lax.axis_index("pipe")
    place = lax.axis_index("expert")
    x = place // (2 * NY)
    y = lax.rem(place // 2, NY)
    core = lax.rem(place, 2)
    half_of_experts = y // (NY // 2)
    mine = lax.rem(y, 2)
    other = 1 - mine

    def at(dz=0, dx=0, dy=0):
        xx = lax.rem(x + dx + NX, NX)
        yy = lax.rem(y + dy + NY, NY)
        return (lax.rem(z + dz + NZ, NZ), (xx * NY + yy) * 2 + core)

    sibling = (z, place + 1 - 2 * core)
    pair = (z, place + 2 - 4 * mine)
    right, left = at(dy=1), at(dy=-1)

    def index_of(offset, parity):
        o = lax.rem(offset + parity + 2 * NY, NY)
        return jnp.where(o == 0, 0, jnp.where(o <= NY // 2, 2 * o - 1, 2 * (NY - o)))

    def index_at(position):
        return position + mine * (1 - 2 * lax.rem(position, 2))

    def offset_at(position):
        ahead = lax.rem(position + mine, 2)
        return (2 * ahead - 1) * ((position + 1) // 2)

    barrier = pltpu.get_barrier_semaphore()
    friends = (right, left, at(dx=1), at(dx=-1), at(dx=2), sibling)
    friends += tuple(at(dz=dz, dy=dy) for dz in (1, -1) for dy in (0, 1, -1))
    for friend in friends:
        pl.semaphore_signal(barrier, inc=1, device_id=friend, device_id_type=MESH)

    inputs = [
        pltpu.make_async_copy(src, dst, in_local.at[number])
        for number, (src, dst) in enumerate(
            (
                (down_hbm, down_ref),
                (up_hbm, up_ref),
                (gains_hbm, gains_ref),
                (router_hbm, router_ref),
                (routes_hbm, routes_ref),
            )
        )
    ]
    for copy in inputs:
        copy.start()

    def remote(src, dst, send, recv, device):
        return pltpu.make_async_remote_copy(
            src_ref=src, dst_ref=dst, send_sem=send, recv_sem=recv, device_id=device, device_id_type=MESH
        )

    def weight_views(index):
        side = index // 2
        if index % 2 == 0:
            return w_up_ref.at[0, side], [wu.at[:, pl.ds((2 * side + o) * HID, HID)] for o in (0, 1)]
        return w_down_ref.at[0, side], [wd.at[pl.ds((2 * side + o) * HID, HID), :] for o in (0, 1)]

    def weight_local(index):
        src, views = weight_views(index)
        return pltpu.make_async_copy(src, views[0], w_local.at[index])

    def weight_remote(index):
        src, views = weight_views(index)
        return remote(src, views[1], w_send.at[index], w_recv.at[index], sibling)

    for index in range(4):
        weight_local(index).start()

    eye = (iota((TOK, TOK), 1) == iota((TOK, TOK), 0)).astype(BF16)
    earlier = (iota((TOK, TOK), 1) < iota((TOK, TOK), 0)).astype(BF16)

    def put(first):
        return (iota((EXPERTS, META), 1) == iota((EXPERTS, META), 0) + first).astype(BF16)

    for copy in inputs:
        copy.wait()
    for side, state_ref in enumerate((down_ref, up_ref)):
        wide = state_ref[0].astype(F32)
        scale_rows = lax.rsqrt(jnp.mean(wide * wide, axis=-1, keepdims=True) + EPSILON)
        normed = (wide * scale_rows * gains_ref[0, side : side + 1, :]).astype(BF16)
        own_rows = slice(side * TOK, (side + 1) * TOK)
        for half in range(2):
            tok[mine, half, own_rows, 0:HALF] = normed[:, half * HALF : (half + 1) * HALF]
        logits = dot_lanes(normed, router_ref[side])
        picked = routes_ref[side]
        named = iota((EXPERTS, TOK), 0)
        hit_rows = ((picked[0:1, :] == named) | (picked[1:2, :] == named)).astype(F32).astype(BF16)
        hit = dot_lanes(eye, hit_rows)
        slot = dot_lanes(earlier, hit_rows)
        affinity = hit * jax.nn.sigmoid(logits)
        weight = ROUTE_SCALE * affinity / jnp.sum(affinity, axis=-1, keepdims=True)
        code = jnp.where(hit > 0.5, slot, -1.0).astype(BF16)
        high = weight.astype(BF16)
        low = (weight - high.astype(F32)).astype(BF16)
        info = dot(code, put(0)) + dot(high, put(EXPERTS)) + dot(low, put(2 * EXPERTS))
        tok[mine, 0, own_rows, HALF:WIDE] = info.astype(BF16)

    pl.semaphore_wait(barrier, len(friends))

    def tok_at(block, half):
        return tok.at[block, half] if half == 0 else tok.at[block, half, :, 0:HALF]

    def own_copy(way, half):
        into = index_of(1 - 2 * way, other)
        return remote(
            tok_at(mine, half), tok_at(into, half), own_send.at[way, half], a_recv.at[into, half],
            right if way else left,
        )

    for half in range(2):
        for way in range(2):
            own_copy(way, half).start()
    for index in range(4):
        weight_remote(index).start()

    zeros_half = jnp.zeros((TOK, HALF), BF16)
    for block in range(BLOCKS):
        back2[block, other] = zeros_half

    rows = 4 * TOK
    row = iota((rows, META), 0)
    expert_of_row = 2 * lax.rem(x + lax.shift_right_logical(row, 4), NX) + half_of_experts
    lane = iota((rows, META), 1)

    def spread(first):
        return (lane == expert_of_row + first).astype(BF16)

    def a_passed(position, half):
        ahead = lax.rem(position + mine, 2)
        last = 2 + (ahead if half else 1 - ahead)
        return (position >= 1) & ((position + 1) // 2 <= last)

    def a_copy(position, half):
        block, offset = index_at(position), offset_at(position)
        way = 1 - 2 * lax.rem(position + mine, 2)
        into = index_of(offset - way, other)
        return remote(
            tok_at(block, half), tok_at(into, half), a_send.at[block, half], a_recv.at[into, half], at(dy=way)
        )

    def a_wait(block, half):
        remote(
            tok_at(block, half), tok_at(block, half), a_send.at[block, half], a_recv.at[block, half], right
        ).wait_recv()

    def b_copy(block, kind, half=0):
        if kind == 2:
            src, dst, number = sel2.at[block, mine], got2.at[block, mine], 4
        else:
            src, dst, number = sel.at[block, kind, half], got.at[block, 1 + kind, half], 2 * kind + half
        return remote(src, dst, b_send.at[block, number], b_recv.at[block, number], at(dx=(1, -1, 2)[kind]))

    def f_copy(block):
        return remote(got2.at[block, mine], got2.at[block, mine], f_send.at[block], f_recv.at[block], pair)

    def f_wait(block):
        remote(
            got2.at[block, other], got2.at[block, other], f_send.at[block], f_recv.at[block], pair
        ).wait_recv()

    def m_copy(block):
        return remote(ans2.at[block, other], mate.at[block], m_send.at[block], m_recv.at[block], pair)

    def d_copy(block, kind, half=0):
        if kind == 2:
            src, dst, number = sum2.at[block], back2.at[block, mine], 4
        else:
            src, dst, number = ans.at[block, kind, half], back.at[block, 1 + kind, half], 2 * kind + half
        return remote(src, dst, d_send.at[block, number], d_recv.at[block, number], at(dx=(-1, 1, 2)[kind]))

    def choose(block, half):
        info = tok[block, 0, :, HALF:WIDE]
        code = dot_lanes(spread(0), info)
        r = iota((rows, 2 * TOK), 0)
        c = iota((rows, 2 * TOK), 1)
        hit = (code == (r & 7).astype(F32)) & ((lax.shift_right_logical(r, 3) & 1) == lax.shift_right_logical(c, 4))
        table = hit.astype(F32).astype(BF16)
        for first in range(0, HALF, TILE):
            span = slice(first, first + TILE)
            picked = dot(table, tok[block, half, :, span]).astype(BF16)
            got[block, 0, half, :, span] = picked[0:TOK]
            sel[block, 0, half, :, span] = picked[TOK : 2 * TOK]
            sel2[block, half, :, span] = picked[2 * TOK : 3 * TOK]
            sel[block, 1, half, :, span] = picked[3 * TOK :]

    def experts(block):
        total = jnp.zeros((rows, 4 * HID), F32)
        for half in range(2):
            lhs = jnp.concatenate(
                [got[block, 0, half], got[block, 1, half], got2[block, half], got[block, 2, half]], axis=0
            )
            total = total + dot(lhs, wu[half * HALF : (half + 1) * HALF, :])
        hidden = total * jax.nn.sigmoid(total)
        r = iota((rows, 4 * HID), 0)
        c = iota((rows, 4 * HID), 1)
        own_side = (lax.shift_right_logical(r, 3) & 1) == lax.shift_right_logical(c, 8)
        hidden = jnp.where(own_side, hidden, 0.0).astype(BF16)
        for half in range(2):
            for first in range(0, HALF, TILE):
                span = slice(first, first + TILE)
                result = dot(hidden, wd[:, half * HALF + first : half * HALF + first + TILE]).astype(BF16)
                back[block, 0, half, :, span] = result[0:TOK]
                ans[block, 0, half, :, span] = result[TOK : 2 * TOK]
                ans2[block, half, :, span] = result[2 * TOK : 3 * TOK]
                ans[block, 1, half, :, span] = result[3 * TOK :]

    def d_near(block, half):
        for kind in range(2):
            d_copy(block, kind, half).start()

    def d_far(block):
        m_copy(block).wait_recv()
        sum2[block] = (ans2[block, mine].astype(F32) + mate[block].astype(F32)).astype(BF16)
        d_copy(block, 2).start()

    def d_whole(block):
        d_near(block, 0)
        d_near(block, 1)
        d_far(block)

    def forward_step(step, carry):
        @pl.when(step < BLOCKS)
        def _():
            block = index_at(step)
            for half in range(2):

                @pl.when(step >= 1)
                def _():
                    a_wait(block, half)

                    @pl.when(a_passed(step, half))
                    def _():
                        a_copy(step, half).start()

                choose(block, half)

                @pl.when(mine == half)
                def _():
                    b_copy(block, 2).start()

                for kind in range(2):
                    b_copy(block, kind, half).start()

        @pl.when((step >= LAG_PASS) & (step < BLOCKS + LAG_PASS))
        def _():
            block = index_at(step - LAG_PASS)
            b_copy(block, 2).wait_recv()
            f_copy(block).start()

        @pl.when(step >= LAG)
        def _():
            block = index_at(step - LAG)

            @pl.when(step == LAG)
            def _():
                for index in range(4):
                    weight_local(index).wait()
                    weight_remote(index).wait_recv()

            for half in range(2):
                for kind in range(2):
                    b_copy(block, kind, half).wait_recv()
            f_wait(block)
            experts(block)
            m_copy(block).start()

            @pl.when(step >= BLOCKS + LAG - 2)
            def _():
                d_near(block, 0)
                d_near(block, 1)

        @pl.when(step == BLOCKS)
        def _():
            d_whole(index_at(FILLER))

        return carry

    lax.fori_loop(0, BLOCKS + LAG, forward_step, 0)

    def combine(block, half):
        for kind in range(2):
            d_copy(block, kind, half).wait_recv()

        @pl.when(mine == half)
        def _():
            d_copy(block, 2).wait_recv()

        info = tok[block, 0, :, HALF:WIDE]
        code = dot_lanes(info, spread(0))
        r = iota((2 * TOK, rows), 0)
        c = iota((2 * TOK, rows), 1)
        hit = (code == (c & 7).astype(F32)) & ((lax.shift_right_logical(c, 3) & 1) == lax.shift_right_logical(r, 4))
        high = jnp.where(hit, dot_lanes(info, spread(EXPERTS)), 0.0).astype(BF16)
        low = jnp.where(hit, dot_lanes(info, spread(2 * EXPERTS)), 0.0).astype(BF16)
        both = jnp.concatenate([high, low], axis=0)
        for first in range(0, HALF, TILE):
            span = slice(first, first + TILE)
            answers = jnp.concatenate(
                [
                    back[block, 0, half, :, span],
                    back[block, 1, half, :, span],
                    back2[block, half, :, span],
                    back[block, 2, half, :, span],
                ],
                axis=0,
            )
            sums = dot(both, answers)
            acc[half, :, span] = sums[0 : 2 * TOK] + sums[2 * TOK :]

    def e_copy(position, half):
        block, offset = index_at(position), offset_at(position)
        ahead = lax.rem(position + mine, 2)
        ahead = jnp.where(position == BLOCKS - 1, 1 - half, ahead)
        way = 2 * ahead - 1
        into = index_of(offset - way, other)
        return remote(
            part.at[block, half], part_in.at[into, half], e_send.at[block, half], e_recv.at[into, half], at(dy=way)
        )

    def e_wait(index, half):
        remote(
            part_in.at[index, half], part_in.at[index, half], e_send.at[0, half], e_recv.at[index, half], right
        ).wait_recv()

    def join(position, half):
        block = index_at(position)
        distance = (position + 1) // 2
        ahead = lax.rem(position + mine, 2)
        combine(block, half)
        joined = (distance <= 2) | ((distance == 3) & (ahead == 1 - half))

        @pl.when(joined)
        def _():
            e_wait(block, half)
            part[block, half] = (acc[half] + part_in[block, half].astype(F32)).astype(BF16)

        @pl.when(jnp.logical_not(joined))
        def _():
            part[block, half] = acc[half].astype(BF16)

    first_z, last_z = z == 0, z == NZ - 1
    stays = (last_z, first_z)
    steps_z = (jnp.where(last_z, 0, 1), jnp.where(first_z, 0, -1))
    results = (jnp.where(last_z, 1, 0), jnp.where(first_z, 0, 1))

    def last_copy(position, half, side):
        block = index_at(position)
        ahead = lax.rem(position + mine, 2)
        result, source = results[side], 2 - ahead
        return remote(
            part.at[block, half, pl.ds(side * TOK, TOK)], fin_in.at[result, source, half],
            l_send.at[position, half, side], z_recv.at[result, source, half],
            at(dz=steps_z[side], dy=2 * ahead - 1),
        )

    def z_copy(side, half):
        return remote(
            fin.at[side, half], fin_in.at[side, 0, half], z_send.at[side, half], z_recv.at[side, 0, half],
            at(dz=1 - 2 * side),
        )

    d_far(index_at(BLOCKS - 1))
    d_far(index_at(BLOCKS - 2))
    for position in range(BLOCKS - 3, -1, -1):
        if position != FILLER:
            d_whole(index_at(position))
    for half in range(2):
        join(BLOCKS - 1, half)
        e_copy(BLOCKS - 1, half).start()

    def backward_step(step, carry):
        distance = NY // 2 - 1 - step

        for half in range(2):
            for position in (2 * distance, 2 * distance - 1):
                join(position, half)
                e_copy(position, half).start()

        return carry

    lax.fori_loop(0, NY // 2 - 2, backward_step, 0)

    for half in range(2):
        for position in (2, 1):
            join(position, half)
            for side in range(2):
                last_copy(position, half, side).start()
        combine(mine, half)
        span = slice(half * HALF, (half + 1) * HALF)
        for side, state_ref in enumerate((down_ref, up_ref)):
            fin[side, half] = (
                state_ref[0, :, span].astype(F32) + acc[half, side * TOK : (side + 1) * TOK]
            ).astype(BF16)

            @pl.when(jnp.logical_not(stays[side]))
            def _():
                z_copy(side, half).start()

            @pl.when(stays[side])
            def _():
                fin_in[1 - side, 0, half] = fin[side, half]

    for half in range(2):
        for way in range(2):
            own_copy(way, half).wait_send()

    for index in range(4):
        weight_remote(index).wait_send()

    def drain(position, carry):
        block = index_at(position)
        for half in range(2):
            for kind in range(2):
                b_copy(block, kind, half).wait_send()
                d_copy(block, kind, half).wait_send()

            @pl.when(a_passed(position, half))
            def _():
                a_copy(position, half).wait_send()

            @pl.when(position >= 3)
            def _():
                e_copy(position, half).wait_send()

        b_copy(block, 2).wait_send()
        d_copy(block, 2).wait_send()
        f_copy(block).wait_send()
        m_copy(block).wait_send()
        return carry

    lax.fori_loop(0, BLOCKS, drain, 0)

    for half in range(2):
        for position in (2, 1):
            for side in range(2):
                last_copy(position, half, side).wait_send()
        span = slice(half * HALF, (half + 1) * HALF)
        for side, out in enumerate((out_down, out_up)):

            @pl.when(jnp.logical_not(stays[side]))
            def _():
                z_copy(side, half).wait_send()

            @pl.when(jnp.logical_not(stays[1 - side]))
            def _():
                z_copy(side, half).wait_recv()

            total = fin_in[side, 0, half].astype(F32)
            for source in (1, 2):
                remote(
                    fin_in.at[side, source, half], fin_in.at[side, source, half],
                    z_send.at[side, half], z_recv.at[side, source, half], right,
                ).wait_recv()
                total = total + fin_in[side, source, half].astype(F32)
            out[0, :, span] = total.astype(BF16)


def on_device(state_down, state_up, routes, gains, router, w_up, w_down):
    vmem = pl.BlockSpec(memory_space=pltpu.VMEM)
    hbm = pl.BlockSpec(memory_space=pl.ANY)
    dma = pltpu.SemaphoreType.DMA
    return pl.pallas_call(
        kernel,
        out_shape=(
            pltpu.VMEM(state_down.shape, BF16),
            pltpu.VMEM(state_up.shape, BF16),
        ),
        in_specs=[hbm] * 7,
        out_specs=(vmem, vmem),
        scratch_shapes=[
            pltpu.VMEM(state_down.shape, BF16),
            pltpu.VMEM(state_up.shape, BF16),
            pltpu.VMEM((2, 2, TOK), jnp.int32),
            pltpu.VMEM(gains.shape, F32),
            pltpu.VMEM((2, EXPERTS, D), BF16),
            dma((5,)),
            pltpu.VMEM((BLOCKS, 2, 2 * TOK, WIDE), BF16),
            pltpu.VMEM((BLOCKS, 2, 2, TOK, HALF), BF16),
            pltpu.VMEM((BLOCKS, 2, TOK, HALF), BF16),
            pltpu.VMEM((BLOCKS, 3, 2, TOK, HALF), BF16),
            pltpu.VMEM((BLOCKS, 2, TOK, HALF), BF16),
            pltpu.VMEM((BLOCKS, 2, 2, TOK, HALF), BF16),
            pltpu.VMEM((BLOCKS, 2, TOK, HALF), BF16),
            pltpu.VMEM((BLOCKS, TOK, HALF), BF16),
            pltpu.VMEM((BLOCKS, TOK, HALF), BF16),
            pltpu.VMEM((BLOCKS, 3, 2, TOK, HALF), BF16),
            pltpu.VMEM((BLOCKS, 2, TOK, HALF), BF16),
            pltpu.VMEM((BLOCKS, 2, 2 * TOK, HALF), BF16),
            pltpu.VMEM((BLOCKS, 2, 2 * TOK, HALF), BF16),
            pltpu.VMEM((2, 2 * TOK, HALF), F32),
            pltpu.VMEM((D, 4 * HID), BF16),
            pltpu.VMEM((4 * HID, D), BF16),
            pltpu.VMEM((2, 2, TOK, HALF), BF16),
            pltpu.VMEM((2, 3, 2, TOK, HALF), BF16),
            dma((2, 2)),
            dma((BLOCKS, 2)),
            dma((BLOCKS, 2)),
            dma((BLOCKS, 5)),
            dma((BLOCKS, 5)),
            dma((BLOCKS,)),
            dma((BLOCKS,)),
            dma((BLOCKS,)),
            dma((BLOCKS,)),
            dma((BLOCKS, 5)),
            dma((BLOCKS, 5)),
            dma((BLOCKS, 2)),
            dma((BLOCKS, 2)),
            dma((3, 2, 2)),
            dma((4,)),
            dma((4,)),
            dma((4,)),
            dma((2, 2)),
            dma((2, 3, 2)),
        ],
        compiler_params=pltpu.CompilerParams(
            collective_id=0, has_side_effects=True, vmem_limit_bytes=56 * 2**20
        ),
        name="routed_experts",
    )(state_down, state_up, jnp.swapaxes(routes[0, 0], 1, 2), gains, jnp.swapaxes(router[0], 1, 2), w_up, w_down)


def solution(mesh):
    in_specs = (
        P("pipe", "expert", None),
        P("pipe", "expert", None),
        P(None, "pipe", None, "expert", None),
        P("pipe", None, None),
        P("pipe", None, None, None),
        P("pipe", None, None, "expert"),
        P("pipe", None, "expert", None),
    )
    out_specs = (P("pipe", "expert", None), P("pipe", "expert", None))
    return jax.shard_map(
        on_device, mesh=mesh, in_specs=in_specs, out_specs=out_specs, check_vma=False
    )
```

```python
import functools

import jax
import jax.numpy as jnp
from jax import lax
from jax.experimental import pallas as pl
from jax.experimental.pallas import tpu as pltpu
from jax.sharding import PartitionSpec as P

MESH = pl.DeviceIdType.MESH
EPSILON = 1e-06
ROUTE_SCALE = 2.5

NX, NY, NZ = 4, 8, 8
EXPERTS = 8
TOK = 16
CAP = 8
D = 3584
HALF = D // 2
META = 128
WIDE = HALF + META
TILE = 256
HID = 128
BLOCKS = NY
LAG_PASS = 2
LAG = 5
FILLER = 3

F32 = jnp.float32
BF16 = jnp.bfloat16


def dot(a, b):
    return jnp.dot(a, b, preferred_element_type=F32)


def dot_lanes(a, b):
    return lax.dot_general(a, b, (((1,), (1,)), ((), ())), preferred_element_type=F32)


def iota(shape, axis):
    return lax.broadcasted_iota(jnp.int32, shape, axis)


def kernel(
    down_hbm, up_hbm, routes_hbm, gains_hbm, router_hbm, w_up_ref, w_down_ref,
    out_down, out_up,
    down_ref, up_ref, routes_ref, gains_ref, router_ref, in_local,
    tok, sel, sel2, got, got2, ans, ans2, mate, sum2, back, back2, part, part_in, acc, wu, wd, fin, fin_in,
    own_send, a_send, a_recv, b_send, b_recv, f_send, f_recv, m_send, m_recv, d_send, d_recv,
    e_send, e_recv, l_send, w_local, w_send, w_recv, z_send, z_recv,
):
    z = lax.axis_index("pipe")
    place = lax.axis_index("expert")
    x = place // (2 * NY)
    y = lax.rem(place // 2, NY)
    core = lax.rem(place, 2)
    half_of_experts = y // (NY // 2)
    mine = lax.rem(y, 2)
    other = 1 - mine

    def at(dz=0, dx=0, dy=0):
        xx = lax.rem(x + dx + NX, NX)
        yy = lax.rem(y + dy + NY, NY)
        return (lax.rem(z + dz + NZ, NZ), (xx * NY + yy) * 2 + core)

    sibling = (z, place + 1 - 2 * core)
    pair = (z, place + 2 - 4 * mine)
    right, left = at(dy=1), at(dy=-1)

    def index_of(offset, parity):
        o = lax.rem(offset + parity + 2 * NY, NY)
        return jnp.where(o == 0, 0, jnp.where(o <= NY // 2, 2 * o - 1, 2 * (NY - o)))

    def index_at(position):
        return position + mine * (1 - 2 * lax.rem(position, 2))

    def offset_at(position):
        ahead = lax.rem(position + mine, 2)
        return (2 * ahead - 1) * ((position + 1) // 2)

    barrier = pltpu.get_barrier_semaphore()
    friends = (right, left, at(dx=1), at(dx=-1), at(dx=2), sibling)
    friends += tuple(at(dz=dz, dy=dy) for dz in (1, -1) for dy in (0, 1, -1))
    for friend in friends:
        pl.semaphore_signal(barrier, inc=1, device_id=friend, device_id_type=MESH)

    inputs = [
        pltpu.make_async_copy(src, dst, in_local.at[number])
        for number, (src, dst) in enumerate(
            (
                (down_hbm, down_ref),
                (up_hbm, up_ref),
                (gains_hbm, gains_ref),
                (router_hbm, router_ref),
                (routes_hbm, routes_ref),
            )
        )
    ]
    for copy in inputs:
        copy.start()

    def remote(src, dst, send, recv, device):
        return pltpu.make_async_remote_copy(
            src_ref=src, dst_ref=dst, send_sem=send, recv_sem=recv, device_id=device, device_id_type=MESH
        )

    def weight_views(index):
        side = index // 2
        if index % 2 == 0:
            return w_up_ref.at[0, side], [wu.at[:, pl.ds((2 * side + o) * HID, HID)] for o in (0, 1)]
        return w_down_ref.at[0, side], [wd.at[pl.ds((2 * side + o) * HID, HID), :] for o in (0, 1)]

    def weight_local(index):
        src, views = weight_views(index)
        return pltpu.make_async_copy(src, views[0], w_local.at[index])

    def weight_remote(index):
        src, views = weight_views(index)
        return remote(src, views[1], w_send.at[index], w_recv.at[index], sibling)

    for index in range(4):
        weight_local(index).start()

    eye = (iota((TOK, TOK), 1) == iota((TOK, TOK), 0)).astype(BF16)
    earlier = (iota((TOK, TOK), 1) < iota((TOK, TOK), 0)).astype(BF16)

    def put(first):
        return (iota((EXPERTS, META), 1) == iota((EXPERTS, META), 0) + first).astype(BF16)

    for copy in inputs:
        copy.wait()
    for side, state_ref in enumerate((down_ref, up_ref)):
        wide = state_ref[0].astype(F32)
        scale_rows = lax.rsqrt(jnp.mean(wide * wide, axis=-1, keepdims=True) + EPSILON)
        normed = (wide * scale_rows * gains_ref[0, side : side + 1, :]).astype(BF16)
        own_rows = slice(side * TOK, (side + 1) * TOK)
        for half in range(2):
            tok[mine, half, own_rows, 0:HALF] = normed[:, half * HALF : (half + 1) * HALF]
        logits = dot_lanes(normed, router_ref[side])
        picked = routes_ref[side]
        named = iota((EXPERTS, TOK), 0)
        hit_rows = ((picked[0:1, :] == named) | (picked[1:2, :] == named)).astype(F32).astype(BF16)
        hit = dot_lanes(eye, hit_rows)
        slot = dot_lanes(earlier, hit_rows)
        affinity = hit * jax.nn.sigmoid(logits)
        weight = ROUTE_SCALE * affinity / jnp.sum(affinity, axis=-1, keepdims=True)
        code = jnp.where(hit > 0.5, slot, -1.0).astype(BF16)
        high = weight.astype(BF16)
        low = (weight - high.astype(F32)).astype(BF16)
        info = dot(code, put(0)) + dot(high, put(EXPERTS)) + dot(low, put(2 * EXPERTS))
        tok[mine, 0, own_rows, HALF:WIDE] = info.astype(BF16)

    zeros_half = jnp.zeros((TOK, HALF), BF16)
    for block in range(BLOCKS):
        back2[block, other] = zeros_half

    pl.semaphore_wait(barrier, len(friends))

    def tok_at(block, half):
        return tok.at[block, half] if half == 0 else tok.at[block, half, :, 0:HALF]

    def own_copy(way, half):
        into = index_of(1 - 2 * way, other)
        return remote(
            tok_at(mine, half), tok_at(into, half), own_send.at[way, half], a_recv.at[into, half],
            right if way else left,
        )

    for half in range(2):
        for way in range(2):
            own_copy(way, half).start()
    for index in range(4):
        weight_remote(index).start()

    rows = 4 * TOK
    row = iota((rows, META), 0)
    expert_of_row = 2 * lax.rem(x + lax.shift_right_logical(row, 4), NX) + half_of_experts
    lane = iota((rows, META), 1)

    def spread(first):
        return (lane == expert_of_row + first).astype(BF16)

    def a_passed(position, half):
        ahead = lax.rem(position + mine, 2)
        last = 2 + (ahead if half else 1 - ahead)
        return (position >= 1) & ((position + 1) // 2 <= last)

    def a_copy(position, half):
        block, offset = index_at(position), offset_at(position)
        way = 1 - 2 * lax.rem(position + mine, 2)
        into = index_of(offset - way, other)
        return remote(
            tok_at(block, half), tok_at(into, half), a_send.at[block, half], a_recv.at[into, half], at(dy=way)
        )

    def a_wait(block, half):
        remote(
            tok_at(block, half), tok_at(block, half), a_send.at[block, half], a_recv.at[block, half], right
        ).wait_recv()

    def b_copy(block, kind, half=0):
        if kind == 2:
            src, dst, number = sel2.at[block, mine], got2.at[block, mine], 4
        else:
            src, dst, number = sel.at[block, kind, half], got.at[block, 1 + kind, half], 2 * kind + half
        return remote(src, dst, b_send.at[block, number], b_recv.at[block, number], at(dx=(1, -1, 2)[kind]))

    def f_copy(block):
        return remote(got2.at[block, mine], got2.at[block, mine], f_send.at[block], f_recv.at[block], pair)

    def f_wait(block):
        remote(
            got2.at[block, other], got2.at[block, other], f_send.at[block], f_recv.at[block], pair
        ).wait_recv()

    def m_copy(block):
        return remote(ans2.at[block, other], mate.at[block], m_send.at[block], m_recv.at[block], pair)

    def d_copy(block, kind, half=0):
        if kind == 2:
            src, dst, number = sum2.at[block], back2.at[block, mine], 4
        else:
            src, dst, number = ans.at[block, kind, half], back.at[block, 1 + kind, half], 2 * kind + half
        return remote(src, dst, d_send.at[block, number], d_recv.at[block, number], at(dx=(-1, 1, 2)[kind]))

    def choose(block, half):
        info = tok[block, 0, :, HALF:WIDE]
        code = dot_lanes(spread(0), info)
        r = iota((rows, 2 * TOK), 0)
        c = iota((rows, 2 * TOK), 1)
        hit = (code == (r & 7).astype(F32)) & ((lax.shift_right_logical(r, 3) & 1) == lax.shift_right_logical(c, 4))
        table = hit.astype(F32).astype(BF16)
        for first in range(0, HALF, TILE):
            span = slice(first, first + TILE)
            picked = dot(table, tok[block, half, :, span]).astype(BF16)
            got[block, 0, half, :, span] = picked[0:TOK]
            sel[block, 0, half, :, span] = picked[TOK : 2 * TOK]
            sel2[block, half, :, span] = picked[2 * TOK : 3 * TOK]
            sel[block, 1, half, :, span] = picked[3 * TOK :]

    def experts(block, at_once):
        total = jnp.zeros((rows, 4 * HID), F32)
        for half in range(2):
            lhs = jnp.concatenate(
                [got[block, 0, half], got[block, 1, half], got2[block, half], got[block, 2, half]], axis=0
            )
            total = total + dot(lhs, wu[half * HALF : (half + 1) * HALF, :])
        hidden = total * jax.nn.sigmoid(total)
        r = iota((rows, 4 * HID), 0)
        c = iota((rows, 4 * HID), 1)
        own_side = (lax.shift_right_logical(r, 3) & 1) == lax.shift_right_logical(c, 8)
        hidden = jnp.where(own_side, hidden, 0.0).astype(BF16)
        for half in range(2):
            for first in range(0, HALF, TILE):
                span = slice(first, first + TILE)
                result = dot(hidden, wd[:, half * HALF + first : half * HALF + first + TILE]).astype(BF16)
                back[block, 0, half, :, span] = result[0:TOK]
                ans[block, 0, half, :, span] = result[TOK : 2 * TOK]
                ans2[block, half, :, span] = result[2 * TOK : 3 * TOK]
                ans[block, 1, half, :, span] = result[3 * TOK :]

            @pl.when(other == half)
            def _():
                m_copy(block).start()

            @pl.when(at_once)
            def _():
                d_near(block, half)

    def d_near(block, half):
        for kind in range(2):
            d_copy(block, kind, half).start()

    def d_far(block):
        m_copy(block).wait_recv()
        sum2[block] = (ans2[block, mine].astype(F32) + mate[block].astype(F32)).astype(BF16)
        d_copy(block, 2).start()

    def d_whole(block):
        d_near(block, 0)
        d_near(block, 1)
        d_far(block)

    def forward_step(step, carry):
        @pl.when(step < BLOCKS)
        def _():
            block = index_at(step)
            for half in range(2):

                @pl.when(step >= 1)
                def _():
                    a_wait(block, half)

                    @pl.when(a_passed(step, half))
                    def _():
                        a_copy(step, half).start()

                choose(block, half)

                @pl.when(mine == half)
                def _():
                    b_copy(block, 2).start()

                for kind in range(2):
                    b_copy(block, kind, half).start()

        @pl.when((step >= LAG_PASS) & (step < BLOCKS + LAG_PASS))
        def _():
            block = index_at(step - LAG_PASS)
            b_copy(block, 2).wait_recv()
            f_copy(block).start()

        @pl.when(step >= LAG)
        def _():
            block = index_at(step - LAG)

            @pl.when(step == LAG)
            def _():
                for index in range(4):
                    weight_local(index).wait()
                    weight_remote(index).wait_recv()

            for half in range(2):
                for kind in range(2):
                    b_copy(block, kind, half).wait_recv()
            f_wait(block)
            experts(block, step >= BLOCKS + LAG - 2)

        @pl.when(step == BLOCKS)
        def _():
            d_whole(index_at(FILLER))

        return carry

    lax.fori_loop(0, BLOCKS + LAG, forward_step, 0)

    def combine(block, half):
        for kind in range(2):
            d_copy(block, kind, half).wait_recv()

        @pl.when(mine == half)
        def _():
            d_copy(block, 2).wait_recv()

        info = tok[block, 0, :, HALF:WIDE]
        code = dot_lanes(info, spread(0))
        r = iota((2 * TOK, rows), 0)
        c = iota((2 * TOK, rows), 1)
        hit = (code == (c & 7).astype(F32)) & ((lax.shift_right_logical(c, 3) & 1) == lax.shift_right_logical(r, 4))
        high = jnp.where(hit, dot_lanes(info, spread(EXPERTS)), 0.0).astype(BF16)
        low = jnp.where(hit, dot_lanes(info, spread(2 * EXPERTS)), 0.0).astype(BF16)
        both = jnp.concatenate([high, low], axis=0)
        for first in range(0, HALF, TILE):
            span = slice(first, first + TILE)
            answers = jnp.concatenate(
                [
                    back[block, 0, half, :, span],
                    back[block, 1, half, :, span],
                    back2[block, half, :, span],
                    back[block, 2, half, :, span],
                ],
                axis=0,
            )
            sums = dot(both, answers)
            acc[half, :, span] = sums[0 : 2 * TOK] + sums[2 * TOK :]

    def e_copy(position, half):
        block, offset = index_at(position), offset_at(position)
        ahead = lax.rem(position + mine, 2)
        ahead = jnp.where(position == BLOCKS - 1, 1 - half, ahead)
        way = 2 * ahead - 1
        into = index_of(offset - way, other)
        return remote(
            part.at[block, half], part_in.at[into, half], e_send.at[block, half], e_recv.at[into, half], at(dy=way)
        )

    def e_wait(index, half):
        remote(
            part_in.at[index, half], part_in.at[index, half], e_send.at[0, half], e_recv.at[index, half], right
        ).wait_recv()

    def join(position, half):
        block = index_at(position)
        distance = (position + 1) // 2
        ahead = lax.rem(position + mine, 2)
        combine(block, half)
        joined = (distance <= 2) | ((distance == 3) & (ahead == 1 - half))

        @pl.when(joined)
        def _():
            e_wait(block, half)
            part[block, half] = (acc[half] + part_in[block, half].astype(F32)).astype(BF16)

        @pl.when(jnp.logical_not(joined))
        def _():
            part[block, half] = acc[half].astype(BF16)

    first_z, last_z = z == 0, z == NZ - 1
    stays = (last_z, first_z)
    steps_z = (jnp.where(last_z, 0, 1), jnp.where(first_z, 0, -1))
    results = (jnp.where(last_z, 1, 0), jnp.where(first_z, 0, 1))

    def last_copy(position, half, side):
        block = index_at(position)
        ahead = lax.rem(position + mine, 2)
        result, source = results[side], 2 - ahead
        return remote(
            part.at[block, half, pl.ds(side * TOK, TOK)], fin_in.at[result, source, half],
            l_send.at[position, half, side], z_recv.at[result, source, half],
            at(dz=steps_z[side], dy=2 * ahead - 1),
        )

    def z_copy(side, half):
        return remote(
            fin.at[side, half], fin_in.at[side, 0, half], z_send.at[side, half], z_recv.at[side, 0, half],
            at(dz=1 - 2 * side),
        )

    d_far(index_at(BLOCKS - 1))
    d_far(index_at(BLOCKS - 2))
    for position in range(BLOCKS - 3, -1, -1):
        if position != FILLER:
            d_whole(index_at(position))
    for half in range(2):
        join(BLOCKS - 1, half)
        e_copy(BLOCKS - 1, half).start()

    def backward_step(step, carry):
        distance = NY // 2 - 1 - step

        for half in range(2):
            for position in (2 * distance, 2 * distance - 1):
                join(position, half)
                e_copy(position, half).start()

        return carry

    lax.fori_loop(0, NY // 2 - 2, backward_step, 0)

    for half in range(2):
        for position in (2, 1):
            join(position, half)
            for side in range(2):
                last_copy(position, half, side).start()
        combine(mine, half)
        span = slice(half * HALF, (half + 1) * HALF)
        for side, state_ref in enumerate((down_ref, up_ref)):
            fin[side, half] = (
                state_ref[0, :, span].astype(F32) + acc[half, side * TOK : (side + 1) * TOK]
            ).astype(BF16)

            @pl.when(jnp.logical_not(stays[side]))
            def _():
                z_copy(side, half).start()

            @pl.when(stays[side])
            def _():
                fin_in[1 - side, 0, half] = fin[side, half]

    for half in range(2):
        for way in range(2):
            own_copy(way, half).wait_send()

    for index in range(4):
        weight_remote(index).wait_send()

    def drain(position, carry):
        block = index_at(position)
        for half in range(2):
            for kind in range(2):
                b_copy(block, kind, half).wait_send()
                d_copy(block, kind, half).wait_send()

            @pl.when(a_passed(position, half))
            def _():
                a_copy(position, half).wait_send()

            @pl.when(position >= 3)
            def _():
                e_copy(position, half).wait_send()

        b_copy(block, 2).wait_send()
        d_copy(block, 2).wait_send()
        f_copy(block).wait_send()
        m_copy(block).wait_send()
        return carry

    lax.fori_loop(0, BLOCKS, drain, 0)

    for half in range(2):
        for position in (2, 1):
            for side in range(2):
                last_copy(position, half, side).wait_send()
        span = slice(half * HALF, (half + 1) * HALF)
        for side, out in enumerate((out_down, out_up)):

            @pl.when(jnp.logical_not(stays[side]))
            def _():
                z_copy(side, half).wait_send()

            @pl.when(jnp.logical_not(stays[1 - side]))
            def _():
                z_copy(side, half).wait_recv()

            total = fin_in[side, 0, half].astype(F32)
            for source in (1, 2):
                remote(
                    fin_in.at[side, source, half], fin_in.at[side, source, half],
                    z_send.at[side, half], z_recv.at[side, source, half], right,
                ).wait_recv()
                total = total + fin_in[side, source, half].astype(F32)
            out[0, :, span] = total.astype(BF16)


def on_device(state_down, state_up, routes, gains, router, w_up, w_down):
    vmem = pl.BlockSpec(memory_space=pltpu.VMEM)
    hbm = pl.BlockSpec(memory_space=pl.ANY)
    dma = pltpu.SemaphoreType.DMA
    return pl.pallas_call(
        kernel,
        out_shape=(
            pltpu.VMEM(state_down.shape, BF16),
            pltpu.VMEM(state_up.shape, BF16),
        ),
        in_specs=[hbm] * 7,
        out_specs=(vmem, vmem),
        scratch_shapes=[
            pltpu.VMEM(state_down.shape, BF16),
            pltpu.VMEM(state_up.shape, BF16),
            pltpu.VMEM((2, 2, TOK), jnp.int32),
            pltpu.VMEM(gains.shape, F32),
            pltpu.VMEM((2, EXPERTS, D), BF16),
            dma((5,)),
            pltpu.VMEM((BLOCKS, 2, 2 * TOK, WIDE), BF16),
            pltpu.VMEM((BLOCKS, 2, 2, TOK, HALF), BF16),
            pltpu.VMEM((BLOCKS, 2, TOK, HALF), BF16),
            pltpu.VMEM((BLOCKS, 3, 2, TOK, HALF), BF16),
            pltpu.VMEM((BLOCKS, 2, TOK, HALF), BF16),
            pltpu.VMEM((BLOCKS, 2, 2, TOK, HALF), BF16),
            pltpu.VMEM((BLOCKS, 2, TOK, HALF), BF16),
            pltpu.VMEM((BLOCKS, TOK, HALF), BF16),
            pltpu.VMEM((BLOCKS, TOK, HALF), BF16),
            pltpu.VMEM((BLOCKS, 3, 2, TOK, HALF), BF16),
            pltpu.VMEM((BLOCKS, 2, TOK, HALF), BF16),
            pltpu.VMEM((BLOCKS, 2, 2 * TOK, HALF), BF16),
            pltpu.VMEM((BLOCKS, 2, 2 * TOK, HALF), BF16),
            pltpu.VMEM((2, 2 * TOK, HALF), F32),
            pltpu.VMEM((D, 4 * HID), BF16),
            pltpu.VMEM((4 * HID, D), BF16),
            pltpu.VMEM((2, 2, TOK, HALF), BF16),
            pltpu.VMEM((2, 3, 2, TOK, HALF), BF16),
            dma((2, 2)),
            dma((BLOCKS, 2)),
            dma((BLOCKS, 2)),
            dma((BLOCKS, 5)),
            dma((BLOCKS, 5)),
            dma((BLOCKS,)),
            dma((BLOCKS,)),
            dma((BLOCKS,)),
            dma((BLOCKS,)),
            dma((BLOCKS, 5)),
            dma((BLOCKS, 5)),
            dma((BLOCKS, 2)),
            dma((BLOCKS, 2)),
            dma((3, 2, 2)),
            dma((4,)),
            dma((4,)),
            dma((4,)),
            dma((2, 2)),
            dma((2, 3, 2)),
        ],
        compiler_params=pltpu.CompilerParams(
            collective_id=0, has_side_effects=True, vmem_limit_bytes=56 * 2**20
        ),
        name="routed_experts",
    )(state_down, state_up, jnp.swapaxes(routes[0, 0], 1, 2), gains, jnp.swapaxes(router[0], 1, 2), w_up, w_down)


def solution(mesh):
    in_specs = (
        P("pipe", "expert", None),
        P("pipe", "expert", None),
        P(None, "pipe", None, "expert", None),
        P("pipe", None, None),
        P("pipe", None, None, None),
        P("pipe", None, None, "expert"),
        P("pipe", None, "expert", None),
    )
    out_specs = (P("pipe", "expert", None), P("pipe", "expert", None))
    return jax.shard_map(
        on_device, mesh=mesh, in_specs=in_specs, out_specs=out_specs, check_vma=False
    )
```
